32 devices in a mesh: lon: 16 (over z, x, core), lat: 2 (over y).
Axes of the slice: x: 2, y: 2, z: 4, core: 2. Of those that a mesh axis runs over, the one named last changes fastest.
Arguments:
- state: float32 [3, 256, 16, 4096], P(None, None, 'lat', 'lon'), may hold values from -6 to 6
- bathymetry: float32 [16, 4096], P('lat', 'lon'), may hold values from 0.5 to 2
- obs_index: int32 [2, 16, 256], P('lat', 'lon'), may hold values from 0 to 2047
- obs_count: int32 [2, 16], P('lat', 'lon'), may hold values from 85 to 256, as said below
- obs_value: float32 [2, 16, 256], P('lat', 'lon'), may hold values from -6 to 6
- obs_sd: float32 [2, 16, 256], P('lat', 'lon'), may hold values from 0.5 to 2
Outputs:
- analysis: float32 [3, 256, 16, 4096], P(None, None, 'lat', 'lon')
The draws below stay inside these ranges and needn't reach their ends.
Inputs may be any that keep to these rules, and one draw needn't show every extreme that they name: `obs_count`: at least 85 slots of every tile are used; at least one tile uses all 256. `obs_index`: several slots may name the same cell.
All inputs are finite; a program needn't handle non-finite values.
Results may differ from the reference program's by a relative error of at most 0.000051.
Values sent between devices are 32-bit elements; how exact they have to be, the bound alone decides.
A program may use at most 128 MiB of HBM per device.

```python
import math
import jax
import jax.numpy as jnp
from jax import lax

M = 256
CLAT = 8
CLON = 256
KOBS = 256
TLAT = 2
TLON = 16
NLAT = 16
NLON = 4096
NOBS = 8192


def draw_obs_count(key, part):
    first, second = jax.random.split(jax.random.fold_in(key, 17))
    counts = jax.random.randint(first, (TLAT * TLON,), KOBS // 3, KOBS + 1)
    spot = jax.random.randint(second, (), 0, TLAT * TLON)
    counts = jnp.where(jnp.arange(TLAT * TLON) == spot, KOBS, counts)
    return counts.reshape(TLAT, TLON).astype(jnp.int32)


def place_ends(array, rng, least, high):
    longest = array.shape.index(max(array.shape))
    spots = []
    for shift in (0, 1):
        where = [jax.random.randint(jax.random.fold_in(rng, axis), (), 0, length) for axis, length in enumerate(array.shape)]
        where[longest] = (where[longest] + shift) % array.shape[longest]
        spots.append(tuple(where))
    return array.at[spots[0]].set(least).at[spots[1]].set(high)


def level_of(key, extent, cuts, smallest, top_value):
    loudness, own = 1.0, jax.random.fold_in(key, 6)
    for dim, shards_of in cuts:
        steps = jnp.exp(jax.random.uniform(jax.random.fold_in(own, dim), (shards_of,), jnp.float32, smallest / len(cuts), top_value / len(cuts)))
        loudness = loudness * jnp.repeat(steps, extent[dim] // shards_of).reshape([-1 if axis == dim else 1 for axis in range(len(extent))])
    return loudness


def noise(rng, shape, spread, bound, cuts=(), kind=jnp.bfloat16):
    values = spread * jax.random.normal(rng, shape, jnp.float32)
    if cuts:
        values = values * level_of(rng, shape, cuts, -0.22, 0.18)
    return jnp.clip(values, -bound, bound).astype(kind)


def setup_inputs(seed: int = 0) -> dict:
    arg_keys = jax.random.split(jax.random.key(seed), 7)
    return {
        "state": noise(arg_keys[0], (3, M, NLAT, NLON), 1.0, 6.0, ((2, 2), (3, 16)), jnp.float32),
        "bathymetry": jnp.clip(jnp.exp(math.log(2.0) - 1.3862944 * jax.random.uniform(arg_keys[1], (NLAT, NLON), jnp.float32) ** level_of(arg_keys[1], (NLAT, NLON), ((0, 2), (1, 16)), -0.2, 0.2)), 0.5, 2.0),
        "obs_index": place_ends(jax.random.randint(arg_keys[2], (TLAT, TLON, KOBS), 0, CLAT * CLON), jax.random.fold_in(arg_keys[2], 1), 0, (CLAT * CLON) - 1).astype(jnp.int32),
        "obs_count": draw_obs_count(jax.random.fold_in(arg_keys[6], 71), 0),
        "obs_value": noise(arg_keys[4], (TLAT, TLON, KOBS), 1.0, 6.0, ((0, 2), (1, 16)), jnp.float32),
        "obs_sd": jnp.clip(jnp.exp(math.log(2.0) - 1.3862944 * jax.random.uniform(arg_keys[5], (TLAT, TLON, KOBS), jnp.float32) ** level_of(arg_keys[5], (TLAT, TLON, KOBS), ((0, 2), (1, 16)), -0.2, 0.2)), 0.5, 2.0),
    }


def pad_rim(field):
    wrapped = jnp.concatenate([field[..., -1:], field, field[..., :1]], axis=-1)
    widths = [(0, 0)] * (field.ndim - 2) + [(1, 1), (0, 0)]
    return jnp.pad(wrapped, widths)

def reference(state, bathymetry, obs_index, obs_count, obs_value, obs_sd):
    rows = jnp.arange(NLAT).astype(jnp.float32)
    fcor = jnp.sin(math.pi / 3.0 * ((rows + 0.5) / NLAT - 0.5))[:, None]
    height, east, north = (state[0], state[1], state[2])
    for step in range(2):
        flux_x = pad_rim(bathymetry * east)
        flux_y = pad_rim(bathymetry * north)
        div = flux_x[:, 1:-1, 2:] - flux_x[:, 1:-1, :-2] + flux_y[:, 2:, 1:-1] - flux_y[:, :-2, 1:-1]
        height = height - 0.25 * div
        wide = pad_rim(height)
        grad_x = wide[:, 1:-1, 2:] - wide[:, 1:-1, :-2]
        grad_y = wide[:, 2:, 1:-1] - wide[:, :-2, 1:-1]
        east_new = east + 0.5 * (fcor * north - 0.5 * grad_x)
        north_new = north + 0.5 * (-fcor * east - 0.5 * grad_y)
        east, north = (east_new, north_new)
    lat_rows = jnp.arange(TLAT, dtype=jnp.int32)[:, None, None] * CLAT + obs_index // CLON
    lon_cols = jnp.arange(TLON, dtype=jnp.int32)[None, :, None] * CLON + obs_index % CLON
    hx = height[:, lat_rows, lon_cols].reshape(M, -1)
    valid = (jnp.arange(KOBS, dtype=jnp.int32)[None, None, :] < obs_count[:, :, None]).astype(jnp.float32).reshape(-1)
    sigma = obs_sd.reshape(-1) * (math.sqrt(NOBS) / 16.0)
    hmean = lax.optimization_barrier(jnp.mean(hx, axis=0))
    anomal = (hx - hmean) / (math.sqrt(M - 1) * sigma) * valid
    innov = (obs_value.reshape(-1) - hmean) / sigma * valid
    gram = jnp.dot(anomal, anomal.T, precision=lax.Precision.HIGHEST)
    proj = jnp.dot(anomal, innov, precision=lax.Precision.HIGHEST)
    eye = jnp.eye(M, dtype=jnp.float32)
    lower = jnp.linalg.cholesky(gram + eye)
    inv_lower = jax.scipy.linalg.solve_triangular(lower, eye, lower=True)
    weights = jax.scipy.linalg.cho_solve((lower, True), proj)
    transform = inv_lower.T + weights[:, None] / math.sqrt(M - 1)
    fields = jnp.stack([height, east, north])
    center = lax.optimization_barrier(jnp.mean(fields, axis=1, keepdims=True))
    mixed = jnp.einsum('nm,cnab->cmab', transform, fields - center, precision=lax.Precision.HIGHEST)
    return center + mixed
```

```python
import functools
import math

import jax
import jax.numpy as jnp
from jax import lax
from jax.experimental import pallas as pl
from jax.experimental.pallas import tpu as pltpu
from jax.sharding import PartitionSpec as P

MESH = pl.DeviceIdType.MESH
PAD = 8


def forecast_kernel(nlon, nlat, members, rows, cols, state, bath, index, count, value, sd, fh, fu, fv,
                    pay, raw, hp, fxp, fy, brep, rbuf, csend, crecv, hx, lsem, rs, rr, cs, cr):
    lon, lat = lax.axis_index("lon"), lax.axis_index("lat")
    west, east = lax.rem(lon + nlon - 1, nlon), lax.rem(lon + 1, nlon)
    last = rows - 1
    has_n, has_s = lat > 0, lat < nlat - 1

    tiles = cols // 128
    loads = [[pltpu.make_async_copy(state.at[c, :, pl.ds(128 * i, 128)], raw.at[c, i], lsem.at[c, i])
              for i in range(tiles)] for c in range(3)]
    for c in (2, 1, 0):
        for load in loads[c]:
            load.start()
    barrier = pltpu.get_barrier_semaphore()
    for side in (west, east):
        pl.semaphore_signal(barrier, inc=1, device_id={"lon": side}, device_id_type=MESH)

    @pl.when(has_n)
    def _():
        pl.semaphore_signal(barrier, inc=1, device_id={"lat": lat - 1}, device_id_type=MESH)

    @pl.when(has_s)
    def _():
        pl.semaphore_signal(barrier, inc=1, device_id={"lat": lat + 1}, device_id_type=MESH)

    bt = bath[...].T
    for r in range(rows):
        brep[r] = jnp.broadcast_to(bt[:, r:r + 1], (cols, 128))
    zero = jnp.zeros((cols, members), jnp.float32)

    @pl.when(jnp.logical_not(has_n))
    def _():
        for e in range(4):
            rbuf[e, 0] = zero

    @pl.when(jnp.logical_not(has_s))
    def _():
        for e in range(4):
            rbuf[e, 1] = zero

    pl.semaphore_wait(barrier, 2 + jnp.minimum(lat, 1) + jnp.minimum(nlat - 1 - lat, 1))

    def row_copy(e, north):
        if e % 2 == 0:
            src = fy.at[0 if north else last]
        else:
            src = hp.at[0 if north else last, pl.ds(PAD, cols)]
        return pltpu.make_async_remote_copy(
            src_ref=src, dst_ref=rbuf.at[e, 1 if north else 0],
            send_sem=rs.at[e, 0 if north else 1], recv_sem=rr.at[e, 1 if north else 0],
            device_id={"lat": lat - 1 if north else lat + 1}, device_id_type=MESH)

    def row_recv(e, side):
        return pltpu.make_async_remote_copy(
            src_ref=rbuf.at[e, side], dst_ref=rbuf.at[e, side], send_sem=rs.at[e, side],
            recv_sem=rr.at[e, side], device_id={"lat": lat - 1 if side == 0 else lat + 1},
            device_id_type=MESH)

    def send_rows(e):
        @pl.when(has_n)
        def _():
            row_copy(e, True).start()

        @pl.when(has_s)
        def _():
            row_copy(e, False).start()

    def wait_rows(e):
        @pl.when(has_n)
        def _():
            row_copy(e, True).wait_send()
            row_recv(e, 0).wait_recv()

        @pl.when(has_s)
        def _():
            row_copy(e, False).wait_send()
            row_recv(e, 1).wait_recv()

    def col_copy(e, side):
        return pltpu.make_async_remote_copy(
            src_ref=csend.at[e, side], dst_ref=crecv.at[e, 1 - side],
            send_sem=cs.at[e, side], recv_sem=cr.at[e, 1 - side],
            device_id={"lon": west if side == 0 else east}, device_id_type=MESH)

    def send_cols(e, ref):
        for r in range(rows):
            csend[e, 0, r:r + 1, :] = ref[r, PAD:PAD + 1, :]
            csend[e, 1, r:r + 1, :] = ref[r, PAD + cols - 1:PAD + cols, :]
        col_copy(e, 0).start()
        col_copy(e, 1).start()

    def wait_cols(e, ref):
        for side in (0, 1):
            col_copy(e, side).wait()
        for r in range(rows):
            ref[r, PAD - 1:PAD, :] = crecv[e, 0, r:r + 1, :]
            ref[r, PAD + cols:PAD + cols + 1, :] = crecv[e, 1, r:r + 1, :]

    def slab(c, r):
        return jnp.concatenate(
            [raw[c, i, pl.ds(r, members, stride=rows), :].T for i in range(tiles)], axis=0)

    def bmul(r, x):
        b = brep[r]
        return jnp.concatenate([x[:, i:i + 128] * b for i in range(0, members, 128)], axis=1)

    def dcol(ref, r):
        return ref[r, PAD + 1:PAD + cols + 1, :] - ref[r, PAD - 1:PAD + cols - 1, :]

    def fcor(r):
        row = (lat * rows + r).astype(jnp.float32)
        angle = jnp.full((1, members), (row + 0.5) / (rows * nlat) - 0.5, jnp.float32)
        return jnp.sin(math.pi / 3.0 * angle)

    for load in loads[2]:
        load.wait()
    for r in (0, last):
        v = slab(2, r)
        fv[r] = v
        fy[r] = bmul(r, v)
    send_rows(0)
    for load in loads[1]:
        load.wait()
    for r in range(rows):
        u = slab(1, r)
        fu[r] = u
        fxp[r, PAD:PAD + cols, :] = bmul(r, u)
    send_cols(0, fxp)
    for r in range(1, last):
        v = slab(2, r)
        fv[r] = v
        fy[r] = bmul(r, v)
    for load in loads[0]:
        load.wait()
    for r in range(rows):
        hp[r, PAD:PAD + cols, :] = slab(0, r)

    def height(r, up, down):
        div = dcol(fxp, r) + down - up
        hp[r, PAD:PAD + cols, :] = hp[r, PAD:PAD + cols, :] - 0.25 * div

    def wind(r, up, down, flux):
        f = fcor(r)
        u, v = fu[r], fv[r]
        un = u + 0.5 * (f * v - 0.5 * dcol(hp, r))
        vn = v - 0.5 * (f * u + 0.5 * (down - up))
        fu[r] = un
        fv[r] = vn
        if flux:
            fxp[r, PAD:PAD + cols, :] = bmul(r, un)
            fy[r] = bmul(r, vn)

    def hrow(r):
        return hp[r, PAD:PAD + cols, :]

    for step in range(2):
        e = 2 * step
        wait_cols(e, fxp)
        if step == 1:
            @pl.loop(1, last)
            def _(r):
                height(r, fy[r - 1], fy[r + 1])
        wait_rows(e)
        height(0, rbuf[e, 0], fy[1])
        height(last, fy[last - 1], rbuf[e, 1])
        send_rows(e + 1)
        if step == 0:
            @pl.loop(1, last)
            def _(r):
                height(r, fy[r - 1], fy[r + 1])
        send_cols(e + 1, hp)
        if step == 1:
            slots = hx.shape[0]

            @pl.loop(0, slots // 8)
            def _(t):
                parts = []
                for k in range(8):
                    cell = index[0, t * 8 + k]
                    parts.append(hp[cell // cols, pl.ds(PAD + lax.rem(cell, cols), 1), :])
                hx[pl.ds(t * 8, 8), :] = jnp.concatenate(parts, axis=0)

            x = hx[...]
            info = jnp.concatenate([value[...], sd[...], jnp.zeros((6, slots), jnp.float32)], axis=0).T
            sigma = info[:, 1:2] * (math.sqrt(slots * nlon * nlat) / 16.0)
            valid = (lax.broadcasted_iota(jnp.int32, (slots, 1), 0) < count[0, 0]).astype(jnp.float32)
            mean = jnp.sum(x, axis=1, keepdims=True) * (1.0 / members)
            yp = (x - mean) * (valid / (math.sqrt(members - 1) * sigma))
            innov = (info[:, 0:1] - mean) * (valid / sigma)
            proj = jnp.sum(yp * innov, axis=0, keepdims=True)
            pay[...] = jnp.dot(yp.T, yp, precision=lax.Precision.HIGHEST,
                               preferred_element_type=jnp.float32)
            half = members // 2
            pay[members - 2:members - 1, 0:half] = proj[:, :half]
            pay[members - 1:members, 0:half] = proj[:, half:]
        wait_cols(e + 1, hp)

        @pl.loop(1, last)
        def _(r):
            wind(r, hrow(r - 1), hrow(r + 1), step == 0)
        wait_rows(e + 1)
        wind(0, rbuf[e + 1, 0], hrow(1), step == 0)
        wind(last, hrow(last - 1), rbuf[e + 1, 1], step == 0)
        if step == 0:
            send_rows(2)
            send_cols(2, fxp)

    for r in range(rows):
        fh[r] = hrow(r)


def forecast(nlon, nlat, state, bathymetry, obs_index, obs_count, obs_value, obs_sd):
    _, members, rows, cols = state.shape
    slots = obs_index.shape[2]
    f32 = jnp.float32
    field = jax.ShapeDtypeStruct((rows, cols, members), f32)
    vmem, smem = pl.BlockSpec(memory_space=pltpu.VMEM), pl.BlockSpec(memory_space=pltpu.SMEM)
    return pl.pallas_call(
        functools.partial(forecast_kernel, nlon, nlat, members, rows, cols),
        out_shape=[field, field, field, jax.ShapeDtypeStruct((members, members), f32)],
        in_specs=[pl.BlockSpec(memory_space=pl.ANY), vmem, smem, smem, vmem, vmem],
        out_specs=[vmem] * 4,
        scratch_shapes=[
            pltpu.VMEM((3, cols // 128, members * rows, 128), f32),
            pltpu.VMEM((rows, cols + 2 * PAD, members), f32),
            pltpu.VMEM((rows, cols + 2 * PAD, members), f32),
            pltpu.VMEM((rows, cols, members), f32),
            pltpu.VMEM((rows, cols, 128), f32),
            pltpu.VMEM((4, 2, cols, members), f32),
            pltpu.VMEM((4, 2, rows, members), f32),
            pltpu.VMEM((4, 2, rows, members), f32),
            pltpu.VMEM((slots, members), f32),
            pltpu.SemaphoreType.DMA((3, cols // 128)),
            pltpu.SemaphoreType.DMA((4, 2)),
            pltpu.SemaphoreType.DMA((4, 2)),
            pltpu.SemaphoreType.DMA((4, 2)),
            pltpu.SemaphoreType.DMA((4, 2)),
        ],
        compiler_params=pltpu.CompilerParams(
            collective_id=0, has_side_effects=True, vmem_limit_bytes=52 * 2**20),
    )(state.reshape(3, members * rows, cols), bathymetry, obs_index.reshape(1, slots), obs_count,
      obs_value.reshape(1, slots), obs_sd.reshape(1, slots))


def sum_kernel(nlon, nlat, size, part, out, other, acc, parts, whole, back, ps, pr, ss, sr, gs, gr, qs, qr):
    lon, lat = lax.axis_index("lon"), lax.axis_index("lat")
    core, pair = lax.rem(lon, 2), lon // 2
    npair = nlon // 2
    peers = npair * nlat
    half = size // 2
    owners = min(peers, half // 8)
    chunk = half // owners
    me = lat * npair + pair
    partner = {"lon": lon + 1 - 2 * core}

    def device(p):
        return {"lon": 2 * lax.rem(p, npair) + core, "lat": p // npair}

    barrier = pltpu.get_barrier_semaphore()
    pl.semaphore_signal(barrier, inc=1, device_id=partner, device_id_type=MESH)

    @pl.loop(1, peers)
    def _(d):
        pl.semaphore_signal(barrier, inc=1, device_id=device(lax.rem(me + d, peers)), device_id_type=MESH)

    pl.semaphore_wait(barrier, peers)
    mine = pl.ds(pl.multiple_of(core * half, half), half)
    theirs = pl.ds(pl.multiple_of((1 - core) * half, half), half)

    def guard(cond, run):
        if owners == peers:
            run()
        else:
            pl.when(cond)(run)

    first = pltpu.make_async_remote_copy(
        src_ref=part.at[theirs], dst_ref=other, send_sem=ps, recv_sem=pr,
        device_id=partner, device_id_type=MESH)
    first.start()
    first.wait()
    acc[...] = part[mine, :] + other[...]

    def scatter(p, frm):
        return pltpu.make_async_remote_copy(
            src_ref=acc.at[pl.ds(pl.multiple_of(p * chunk, chunk), chunk)], dst_ref=parts.at[frm],
            send_sem=ss.at[p], recv_sem=sr.at[frm], device_id=device(p), device_id_type=MESH)

    def arrive(frm):
        return pltpu.make_async_remote_copy(
            src_ref=parts.at[frm], dst_ref=parts.at[frm],
            send_sem=ss.at[0], recv_sem=sr.at[frm], device_id=device(frm), device_id_type=MESH)

    @pl.loop(1, peers)
    def _(d):
        p = lax.rem(me + d, peers)
        guard(p < owners, lambda: scatter(p, me).start())

    def collect():
        total = acc[pl.ds(pl.multiple_of(me * chunk, chunk), chunk), :]

        def body(d, total):
            frm = lax.rem(me + d, peers)
            arrive(frm).wait_recv()
            return total + parts[frm]
        whole[me] = lax.fori_loop(1, peers, body, total)

    guard(me < owners, collect)

    @pl.loop(1, peers)
    def _(d):
        p = lax.rem(me + d, peers)
        guard(p < owners, lambda: scatter(p, me).wait_send())

    def spread(p, frm):
        return pltpu.make_async_remote_copy(
            src_ref=whole.at[frm], dst_ref=whole.at[frm],
            send_sem=gs.at[p], recv_sem=gr.at[frm], device_id=device(p), device_id_type=MESH)

    def send_all():
        @pl.loop(1, peers)
        def _(d):
            p = lax.rem(me + d, peers)
            spread(p, me).start()

    guard(me < owners, send_all)

    @pl.loop(1, peers)
    def _(d):
        p = lax.rem(me + d, peers)
        guard(p < owners, lambda: spread(p, p).wait_recv())

    last = pltpu.make_async_remote_copy(
        src_ref=whole, dst_ref=back, send_sem=qs, recv_sem=qr,
        device_id=partner, device_id_type=MESH)
    last.start()

    def sent_all():
        @pl.loop(1, peers)
        def _(d):
            p = lax.rem(me + d, peers)
            spread(p, me).wait_send()

    guard(me < owners, sent_all)
    out[mine, :] = whole[...].reshape(half, size)
    last.wait()
    out[theirs, :] = back[...].reshape(half, size)


def total_sum(nlon, nlat, part):
    size = part.shape[0]
    half, peers = size // 2, nlon // 2 * nlat
    owners = min(peers, half // 8)
    chunk = half // owners
    f32 = jnp.float32
    dma = pltpu.SemaphoreType.DMA
    vmem = pl.BlockSpec(memory_space=pltpu.VMEM)
    return pl.pallas_call(
        functools.partial(sum_kernel, nlon, nlat, size),
        out_shape=jax.ShapeDtypeStruct((size, size), f32),
        in_specs=[vmem],
        out_specs=vmem,
        scratch_shapes=[
            pltpu.VMEM((half, size), f32), pltpu.VMEM((half, size), f32),
            pltpu.VMEM((peers, chunk, size), f32), pltpu.VMEM((owners, chunk, size), f32),
            pltpu.VMEM((owners, chunk, size), f32),
            dma, dma, dma((peers,)), dma((peers,)), dma((peers,)), dma((peers,)), dma, dma,
        ],
        compiler_params=pltpu.CompilerParams(
            collective_id=1, has_side_effects=True, vmem_limit_bytes=32 * 2**20),
    )(part)


def split(x):
    hi = x.astype(jnp.bfloat16)
    return hi, (x - hi.astype(jnp.float32)).astype(jnp.bfloat16)


def invert(gram, size):
    lane = lax.broadcasted_iota(jnp.int32, (8, size), 1)
    sub = lax.broadcasted_iota(jnp.int32, (8, size), 0)
    sub1 = lax.broadcasted_iota(jnp.int32, (8, 1), 0)
    blocks = [gram[8 * t:8 * t + 8, :] + (lane == sub + 8 * t).astype(jnp.float32)
              for t in range(size // 8)]
    done = []
    for t in range(size // 8):
        base = 8 * t
        row = blocks[t]
        diag = [row[:, base + q:base + q + 1] for q in range(8)]
        inv = jnp.zeros((8, 1), jnp.float32)
        rsq = jnp.zeros((8, 1), jnp.float32)
        for k in range(8):
            pivot = diag[k][k:k + 1, :]
            recip = 1.0 / pivot
            inv = jnp.where(sub1 == k, recip, inv)
            rsq = jnp.where(sub1 == k, lax.rsqrt(pivot), rsq)
            if k < 7:
                f = jnp.where(sub1 > k, diag[k] * recip, 0.0)
                for q in range(k + 1, 8):
                    diag[q] = diag[q] - f * diag[q][k:k + 1, :]
                row = jnp.where((lane == base + k) & (sub > k), -f, row - f * row[k:k + 1, :])
        inpanel = (lane >= base) & (lane < base + 8)
        low = jnp.where(lane == base + sub, 1.0, jnp.where(lane > base + sub, 0.0, row))
        done.append(low * rsq)
        if t + 1 < size // 8:
            used = jnp.where(inpanel, low, row)
            factor = (row * inv).T
            for s in range(t + 1, size // 8):
                fac = factor[8 * s:8 * s + 8, :]
                new = jnp.where(inpanel, 0.0, blocks[s])
                for k in range(8):
                    new = new - fac[:, k:k + 1] * used[k:k + 1, :]
                blocks[s] = new
    return jnp.concatenate(done, axis=0)


def mix_kernel(members, gram, fh, fu, fv, out, hi, lo):
    @pl.when((pl.program_id(0) == 0) & (pl.program_id(1) == 0))
    def _():
        g = gram[...]
        half = members // 2
        proj = jnp.concatenate([g[members - 2:members - 1, :half], g[members - 1:members, :half]], axis=1)
        inv = invert(gram, members)
        part = jnp.sum(inv * proj, axis=1, keepdims=True)
        weights = jnp.sum(inv * part, axis=0, keepdims=True)
        t = inv + weights * (1.0 / math.sqrt(members - 1))
        t = t + (1.0 - jnp.sum(t, axis=1, keepdims=True)) * (1.0 / members)
        a, b = split(t)
        hi[...] = a
        lo[...] = b

    def mix(ref):
        dims = (((1,), (1,)), ((), ()))
        dot = functools.partial(lax.dot_general, dimension_numbers=dims, preferred_element_type=jnp.float32)
        rows = ref.shape[0]
        for r in range(rows):
            a, b = split(ref[r])
            out[0, pl.ds(r, members, stride=rows), :] = (
                dot(hi[...], a) + dot(hi[...], b) + dot(lo[...], a))

    for c, ref in enumerate((fh, fu, fv)):
        pl.when(pl.program_id(0) == c)(functools.partial(mix, ref))


def mixing(gram, fields):
    rows, cols, members = fields[0].shape
    width = 128
    steps = cols // width

    def spec(c):
        return pl.BlockSpec((rows, width, members), lambda i, j: (0, jnp.where(i == c, j, jnp.where(i < c, 0, steps - 1)), 0))

    out = pl.pallas_call(
        functools.partial(mix_kernel, members),
        grid=(3, steps),
        out_shape=jax.ShapeDtypeStruct((3, members * rows, cols), jnp.float32),
        in_specs=[pl.BlockSpec((members, members), lambda i, j: (0, 0))] + [spec(c) for c in range(3)],
        out_specs=pl.BlockSpec((1, members * rows, width), lambda i, j: (i, 0, j)),
        scratch_shapes=[pltpu.VMEM((members, members), jnp.bfloat16)] * 2,
        compiler_params=pltpu.CompilerParams(vmem_limit_bytes=48 * 2**20),
    )(gram, *fields)
    return out.reshape(3, members, rows, cols)


def shards(nlon, nlat, state, bathymetry, obs_index, obs_count, obs_value, obs_sd):
    h, u, v, part = forecast(nlon, nlat, state, bathymetry, obs_index, obs_count, obs_value, obs_sd)
    gram = total_sum(nlon, nlat, part)
    return mixing(gram, (h, u, v))


def solution(mesh):
    return jax.shard_map(
        functools.partial(shards, mesh.shape["lon"], mesh.shape["lat"]),
        mesh=mesh,
        in_specs=(
            P(None, None, "lat", "lon"),
            P("lat", "lon"),
            P("lat", "lon", None),
            P("lat", "lon"),
            P("lat", "lon", None),
            P("lat", "lon", None),
        ),
        out_specs=P(None, None, "lat", "lon"),
        check_vma=False,
    )
```

```python
import functools
import math

import jax
import jax.numpy as jnp
from jax import lax
from jax.experimental import pallas as pl
from jax.experimental.pallas import tpu as pltpu
from jax.sharding import PartitionSpec as P

MESH = pl.DeviceIdType.MESH
PAD = 8


def forecast_kernel(nlon, nlat, members, rows, cols, state, bath_at, index_at, count_at, value_at, sd_at,
                    out_h, out_u, out_v, pay, raw, hp, fu, fv, fxp, fy, brep, rbuf, csend, crecv, hx,
                    bath, index, count, value, sd, lsem, isem, osem, rs, rr, cs, cr):
    lon, lat = lax.axis_index("lon"), lax.axis_index("lat")
    west, east = lax.rem(lon + nlon - 1, nlon), lax.rem(lon + 1, nlon)
    last = rows - 1
    has_n, has_s = lat > 0, lat < nlat - 1

    tiles = cols // 128
    loads = [[pltpu.make_async_copy(state.at[c, :, pl.ds(128 * i, 128)], raw.at[c, i], lsem.at[c, i])
              for i in range(tiles)] for c in range(3)]
    for c in (2, 1, 0):
        for load in loads[c]:
            load.start()
    small = [pltpu.make_async_copy(src, dst, isem.at[i]) for i, (src, dst) in enumerate((
        (bath_at, bath), (index_at, index), (count_at, count), (value_at, value), (sd_at, sd)))]
    for load in small:
        load.start()
    barrier = pltpu.get_barrier_semaphore()
    for side in (west, east):
        pl.semaphore_signal(barrier, inc=1, device_id={"lon": side}, device_id_type=MESH)

    @pl.when(has_n)
    def _():
        pl.semaphore_signal(barrier, inc=1, device_id={"lat": lat - 1}, device_id_type=MESH)

    @pl.when(has_s)
    def _():
        pl.semaphore_signal(barrier, inc=1, device_id={"lat": lat + 1}, device_id_type=MESH)

    small[0].wait()
    bt = bath[...].T
    for r in range(rows):
        brep[r] = jnp.broadcast_to(bt[:, r:r + 1], (cols, 128))
    zero = jnp.zeros((cols, members), jnp.float32)

    @pl.when(jnp.logical_not(has_n))
    def _():
        for e in range(4):
            rbuf[e, 0] = zero

    @pl.when(jnp.logical_not(has_s))
    def _():
        for e in range(4):
            rbuf[e, 1] = zero

    pl.semaphore_wait(barrier, 2 + jnp.minimum(lat, 1) + jnp.minimum(nlat - 1 - lat, 1))

    def row_copy(e, north):
        if e % 2 == 0:
            src = fy.at[0 if north else last]
        else:
            src = hp.at[0 if north else last, pl.ds(PAD, cols)]
        return pltpu.make_async_remote_copy(
            src_ref=src, dst_ref=rbuf.at[e, 1 if north else 0],
            send_sem=rs.at[e, 0 if north else 1], recv_sem=rr.at[e, 1 if north else 0],
            device_id={"lat": lat - 1 if north else lat + 1}, device_id_type=MESH)

    def row_recv(e, side):
        return pltpu.make_async_remote_copy(
            src_ref=rbuf.at[e, side], dst_ref=rbuf.at[e, side], send_sem=rs.at[e, side],
            recv_sem=rr.at[e, side], device_id={"lat": lat - 1 if side == 0 else lat + 1},
            device_id_type=MESH)

    def send_rows(e):
        @pl.when(has_n)
        def _():
            row_copy(e, True).start()

        @pl.when(has_s)
        def _():
            row_copy(e, False).start()

    def wait_rows(e):
        @pl.when(has_n)
        def _():
            row_copy(e, True).wait_send()
            row_recv(e, 0).wait_recv()

        @pl.when(has_s)
        def _():
            row_copy(e, False).wait_send()
            row_recv(e, 1).wait_recv()

    def col_copy(e, side):
        return pltpu.make_async_remote_copy(
            src_ref=csend.at[e, side], dst_ref=crecv.at[e, 1 - side],
            send_sem=cs.at[e, side], recv_sem=cr.at[e, 1 - side],
            device_id={"lon": west if side == 0 else east}, device_id_type=MESH)

    def send_cols(e, ref):
        for r in range(rows):
            csend[e, 0, r:r + 1, :] = ref[r, PAD:PAD + 1, :]
            csend[e, 1, r:r + 1, :] = ref[r, PAD + cols - 1:PAD + cols, :]
        col_copy(e, 0).start()
        col_copy(e, 1).start()

    def wait_cols(e, ref):
        for side in (0, 1):
            col_copy(e, side).wait()
        for r in range(rows):
            ref[r, PAD - 1:PAD, :] = crecv[e, 0, r:r + 1, :]
            ref[r, PAD + cols:PAD + cols + 1, :] = crecv[e, 1, r:r + 1, :]

    def slab(c, r):
        return jnp.concatenate(
            [raw[c, i, pl.ds(r, members, stride=rows), :].T for i in range(tiles)], axis=0)

    def bmul(r, x):
        b = brep[r]
        return jnp.concatenate([x[:, i:i + 128] * b for i in range(0, members, 128)], axis=1)

    def dcol(ref, r):
        return ref[r, PAD + 1:PAD + cols + 1, :] - ref[r, PAD - 1:PAD + cols - 1, :]

    def fcor(r):
        row = (lat * rows + r).astype(jnp.float32)
        angle = jnp.full((1, members), (row + 0.5) / (rows * nlat) - 0.5, jnp.float32)
        return jnp.sin(math.pi / 3.0 * angle)

    for load in loads[2]:
        load.wait()
    for r in (0, last):
        v = slab(2, r)
        fv[r] = v
        fy[r] = bmul(r, v)
    send_rows(0)
    for load in loads[1]:
        load.wait()
    for r in range(rows):
        u = slab(1, r)
        fu[r] = u
        fxp[r, PAD:PAD + cols, :] = bmul(r, u)
    send_cols(0, fxp)
    for r in range(1, last):
        v = slab(2, r)
        fv[r] = v
        fy[r] = bmul(r, v)
    for load in loads[0]:
        load.wait()
    for r in range(rows):
        hp[r, PAD:PAD + cols, :] = slab(0, r)

    def height(r, up, down):
        div = dcol(fxp, r) + down - up
        hp[r, PAD:PAD + cols, :] = hp[r, PAD:PAD + cols, :] - 0.25 * div

    def wind(r, up, down, flux):
        f = fcor(r)
        u, v = fu[r], fv[r]
        un = u + 0.5 * (f * v - 0.5 * dcol(hp, r))
        vn = v - 0.5 * (f * u + 0.5 * (down - up))
        fu[r] = un
        fv[r] = vn
        if flux:
            fxp[r, PAD:PAD + cols, :] = bmul(r, un)
            fy[r] = bmul(r, vn)

    def hrow(r):
        return hp[r, PAD:PAD + cols, :]

    out_copies = [
        pltpu.make_async_copy(hp.at[:, pl.ds(PAD, cols)], out_h, osem.at[0]),
        pltpu.make_async_copy(fu, out_u, osem.at[1]),
        pltpu.make_async_copy(fv, out_v, osem.at[2]),
    ]
    for step in range(2):
        e = 2 * step
        wait_cols(e, fxp)
        if step == 1:
            @pl.loop(1, last)
            def _(r):
                height(r, fy[r - 1], fy[r + 1])
        wait_rows(e)
        height(0, rbuf[e, 0], fy[1])
        height(last, fy[last - 1], rbuf[e, 1])
        send_rows(e + 1)
        if step == 0:
            @pl.loop(1, last)
            def _(r):
                height(r, fy[r - 1], fy[r + 1])
        send_cols(e + 1, hp)
        if step == 1:
            slots = hx.shape[0]
            out_copies[0].start()
            for load in small[1:]:
                load.wait()

            @pl.loop(0, slots // 8)
            def _(t):
                parts = []
                for k in range(8):
                    cell = index[0, t * 8 + k]
                    parts.append(hp[cell // cols, pl.ds(PAD + lax.rem(cell, cols), 1), :])
                hx[pl.ds(t * 8, 8), :] = jnp.concatenate(parts, axis=0)

            x = hx[...]
            info = jnp.concatenate([value[...], sd[...], jnp.zeros((6, slots), jnp.float32)], axis=0).T
            sigma = info[:, 1:2] * (math.sqrt(slots * nlon * nlat) / 16.0)
            valid = (lax.broadcasted_iota(jnp.int32, (slots, 1), 0) < count[0, 0]).astype(jnp.float32)
            mean = jnp.sum(x, axis=1, keepdims=True) * (1.0 / members)
            yp = (x - mean) * (valid / (math.sqrt(members - 1) * sigma))
            innov = (info[:, 0:1] - mean) * (valid / sigma)
            proj = jnp.sum(yp * innov, axis=0, keepdims=True)
            pay[...] = jnp.dot(yp.T, yp, precision=lax.Precision.HIGHEST,
                               preferred_element_type=jnp.float32)
            half = members // 2
            pay[members - 2:members - 1, 0:half] = proj[:, :half]
            pay[members - 1:members, 0:half] = proj[:, half:]
        wait_cols(e + 1, hp)

        @pl.loop(1, last)
        def _(r):
            wind(r, hrow(r - 1), hrow(r + 1), step == 0)
        wait_rows(e + 1)
        wind(0, rbuf[e + 1, 0], hrow(1), step == 0)
        wind(last, hrow(last - 1), rbuf[e + 1, 1], step == 0)
        if step == 0:
            send_rows(2)
            send_cols(2, fxp)

    out_copies[1].start()
    out_copies[2].start()
    for copy in out_copies:
        copy.wait()


def forecast(nlon, nlat, state, bathymetry, obs_index, obs_count, obs_value, obs_sd):
    _, members, rows, cols = state.shape
    slots = obs_index.shape[2]
    f32 = jnp.float32
    field = jax.ShapeDtypeStruct((rows, cols, members), f32)
    vmem, hbm = pl.BlockSpec(memory_space=pltpu.VMEM), pl.BlockSpec(memory_space=pl.ANY)
    return pl.pallas_call(
        functools.partial(forecast_kernel, nlon, nlat, members, rows, cols),
        out_shape=[field, field, field, jax.ShapeDtypeStruct((members, members), f32)],
        in_specs=[hbm] * 6,
        out_specs=[hbm] * 3 + [vmem],
        scratch_shapes=[
            pltpu.VMEM((3, cols // 128, members * rows, 128), f32),
            pltpu.VMEM((rows, cols + 2 * PAD, members), f32),
            pltpu.VMEM((rows, cols, members), f32),
            pltpu.VMEM((rows, cols, members), f32),
            pltpu.VMEM((rows, cols + 2 * PAD, members), f32),
            pltpu.VMEM((rows, cols, members), f32),
            pltpu.VMEM((rows, cols, 128), f32),
            pltpu.VMEM((4, 2, cols, members), f32),
            pltpu.VMEM((4, 2, rows, members), f32),
            pltpu.VMEM((4, 2, rows, members), f32),
            pltpu.VMEM((slots, members), f32),
            pltpu.VMEM((rows, cols), f32),
            pltpu.SMEM((1, slots), jnp.int32),
            pltpu.SMEM((1, 1), jnp.int32),
            pltpu.VMEM((1, slots), f32),
            pltpu.VMEM((1, slots), f32),
            pltpu.SemaphoreType.DMA((3, cols // 128)),
            pltpu.SemaphoreType.DMA((5,)),
            pltpu.SemaphoreType.DMA((3,)),
            pltpu.SemaphoreType.DMA((4, 2)),
            pltpu.SemaphoreType.DMA((4, 2)),
            pltpu.SemaphoreType.DMA((4, 2)),
            pltpu.SemaphoreType.DMA((4, 2)),
        ],
        compiler_params=pltpu.CompilerParams(
            collective_id=0, has_side_effects=True, vmem_limit_bytes=52 * 2**20),
    )(state.reshape(3, members * rows, cols), bathymetry, obs_index.reshape(1, slots), obs_count,
      obs_value.reshape(1, slots), obs_sd.reshape(1, slots))


def sum_kernel(nlon, nlat, size, part, out, other, acc, parts, whole, back, ps, pr, ss, sr, gs, gr, qs, qr):
    lon, lat = lax.axis_index("lon"), lax.axis_index("lat")
    core, pair = lax.rem(lon, 2), lon // 2
    npair = nlon // 2
    peers = npair * nlat
    half = size // 2
    owners = min(peers, half // 8)
    chunk = half // owners
    me = lat * npair + pair
    partner = {"lon": lon + 1 - 2 * core}

    def device(p):
        return {"lon": 2 * lax.rem(p, npair) + core, "lat": p // npair}

    barrier = pltpu.get_barrier_semaphore()
    pl.semaphore_signal(barrier, inc=1, device_id=partner, device_id_type=MESH)

    @pl.loop(1, peers)
    def _(d):
        pl.semaphore_signal(barrier, inc=1, device_id=device(lax.rem(me + d, peers)), device_id_type=MESH)

    pl.semaphore_wait(barrier, peers)
    mine = pl.ds(pl.multiple_of(core * half, half), half)
    theirs = pl.ds(pl.multiple_of((1 - core) * half, half), half)

    def guard(cond, run):
        if owners == peers:
            run()
        else:
            pl.when(cond)(run)

    first = pltpu.make_async_remote_copy(
        src_ref=part.at[theirs], dst_ref=other, send_sem=ps, recv_sem=pr,
        device_id=partner, device_id_type=MESH)
    first.start()
    first.wait()
    acc[...] = part[mine, :] + other[...]

    def scatter(p, frm):
        return pltpu.make_async_remote_copy(
            src_ref=acc.at[pl.ds(pl.multiple_of(p * chunk, chunk), chunk)], dst_ref=parts.at[frm],
            send_sem=ss.at[p], recv_sem=sr.at[frm], device_id=device(p), device_id_type=MESH)

    def arrive(frm):
        return pltpu.make_async_remote_copy(
            src_ref=parts.at[frm], dst_ref=parts.at[frm],
            send_sem=ss.at[0], recv_sem=sr.at[frm], device_id=device(frm), device_id_type=MESH)

    @pl.loop(1, peers)
    def _(d):
        p = lax.rem(me + d, peers)
        guard(p < owners, lambda: scatter(p, me).start())

    def collect():
        total = acc[pl.ds(pl.multiple_of(me * chunk, chunk), chunk), :]

        def body(d, total):
            frm = lax.rem(me + d, peers)
            arrive(frm).wait_recv()
            return total + parts[frm]
        whole[me] = lax.fori_loop(1, peers, body, total)

    guard(me < owners, collect)

    @pl.loop(1, peers)
    def _(d):
        p = lax.rem(me + d, peers)
        guard(p < owners, lambda: scatter(p, me).wait_send())

    def spread(p, frm):
        return pltpu.make_async_remote_copy(
            src_ref=whole.at[frm], dst_ref=whole.at[frm],
            send_sem=gs.at[p], recv_sem=gr.at[frm], device_id=device(p), device_id_type=MESH)

    def send_all():
        @pl.loop(1, peers)
        def _(d):
            p = lax.rem(me + d, peers)
            spread(p, me).start()

    guard(me < owners, send_all)

    @pl.loop(1, peers)
    def _(d):
        p = lax.rem(me + d, peers)
        guard(p < owners, lambda: spread(p, p).wait_recv())

    last = pltpu.make_async_remote_copy(
        src_ref=whole, dst_ref=back, send_sem=qs, recv_sem=qr,
        device_id=partner, device_id_type=MESH)
    last.start()

    def sent_all():
        @pl.loop(1, peers)
        def _(d):
            p = lax.rem(me + d, peers)
            spread(p, me).wait_send()

    guard(me < owners, sent_all)
    out[mine, :] = whole[...].reshape(half, size)
    last.wait()
    out[theirs, :] = back[...].reshape(half, size)


def total_sum(nlon, nlat, part):
    size = part.shape[0]
    half, peers = size // 2, nlon // 2 * nlat
    owners = min(peers, half // 8)
    chunk = half // owners
    f32 = jnp.float32
    dma = pltpu.SemaphoreType.DMA
    vmem = pl.BlockSpec(memory_space=pltpu.VMEM)
    return pl.pallas_call(
        functools.partial(sum_kernel, nlon, nlat, size),
        out_shape=jax.ShapeDtypeStruct((size, size), f32),
        in_specs=[vmem],
        out_specs=vmem,
        scratch_shapes=[
            pltpu.VMEM((half, size), f32), pltpu.VMEM((half, size), f32),
            pltpu.VMEM((peers, chunk, size), f32), pltpu.VMEM((owners, chunk, size), f32),
            pltpu.VMEM((owners, chunk, size), f32),
            dma, dma, dma((peers,)), dma((peers,)), dma((peers,)), dma((peers,)), dma, dma,
        ],
        compiler_params=pltpu.CompilerParams(
            collective_id=1, has_side_effects=True, vmem_limit_bytes=8 * 2**20),
    )(part)


def split(x):
    hi = x.astype(jnp.bfloat16)
    return hi, (x - hi.astype(jnp.float32)).astype(jnp.bfloat16)


def recip(x):
    r = pl.reciprocal(x, approx=True)
    return r * (2.0 - x * r)


def tree_sum(terms):
    while len(terms) > 1:
        terms = [sum(terms[i:i + 2][1:], terms[i]) for i in range(0, len(terms), 2)]
    return terms[0]


def invert_block(x):
    size, step = x.shape[0], 16
    lane = lax.broadcasted_iota(jnp.int32, (step, size), 1)
    sub = lax.broadcasted_iota(jnp.int32, (step, size), 0)
    blocks = [x[i:i + step, :] for i in range(0, size, step)]
    done = []
    for t in range(size // step):
        base = step * t
        row = blocks[t]
        inpanel = (lane >= base) & (lane < base + step)
        diag = [jnp.broadcast_to(row[:, base + q:base + q + 1], (step, size)) for q in range(step)]
        aug = jnp.where(inpanel, jnp.where(lane == base + sub, 1.0, 0.0), row)
        inv = jnp.zeros((step, size), jnp.float32)
        piv = jnp.ones((step, size), jnp.float32)
        for k in range(0, step, 2):
            d0, d1 = diag[k], diag[k + 1]
            a, b, c = d0[k:k + 1, :], d1[k:k + 1, :], d1[k + 1:k + 2, :]
            det = a * c - b * b
            ra, rdet = recip(a), recip(det)
            ratio, rp = b * ra, a * rdet
            inv = jnp.where(sub == k, ra, jnp.where(sub == k + 1, rp, inv))
            piv = jnp.where(sub == k, a, jnp.where(sub == k + 1, det * ra, piv))
            l0 = jnp.where(sub > k, d0 * ra, 0.0)
            l1 = jnp.where(sub > k + 1, (d1 - l0 * b) * rp, 0.0)

            def eliminate(z):
                first = z[k:k + 1, :]
                second = z[k + 1:k + 2, :] - ratio * first
                return z - (l0 * first + l1 * second)

            for q in range(k + 2, step):
                diag[q] = eliminate(diag[q])
            aug = eliminate(aug)
        done.append(jnp.where(lane < base + step, aug, 0.0) * lax.rsqrt(piv))
        if base + step < size:
            factor = (aug * inv).T
            for s in range(t + 1, size // step):
                fac = factor[step * s:step * (s + 1), :]
                terms = [fac[:, k:k + 1] * aug[k:k + 1, :] for k in range(step)]
                blocks[s] = jnp.where(inpanel, 0.0, blocks[s]) - tree_sum(terms)
    return jnp.concatenate(done, axis=0)


def dot_at(x, y, dims):
    return lax.dot_general(x, y, (dims, ((), ())), precision=lax.Precision.HIGHEST,
                           preferred_element_type=jnp.float32)


def invert(gram):
    size = gram.shape[0]
    half = size // 2
    i = lax.broadcasted_iota(jnp.int32, (half, half), 0)
    j = lax.broadcasted_iota(jnp.int32, (half, half), 1)
    eye = (i == j).astype(jnp.float32)
    m1 = invert_block(gram[:half, :half] + eye)
    side = dot_at(m1, gram[:half, half:], ((1,), (0,)))
    st = side.T
    m2 = invert_block(gram[half:, half:] + eye - dot_at(st, side, ((1,), (0,))))
    low = -dot_at(m2, dot_at(st, m1, ((1,), (0,))), ((1,), (0,)))
    top = jnp.concatenate([m1, jnp.zeros((half, half), jnp.float32)], axis=1)
    return jnp.concatenate([top, jnp.concatenate([low, m2], axis=1)], axis=0)


def factor_kernel(members, gram, hi, lo):
    g = gram[...]
    half = members // 2
    proj = jnp.concatenate([g[members - 2:members - 1, :half], g[members - 1:members, :half]], axis=1)
    inv = invert(g)
    part = jnp.sum(inv * proj, axis=1, keepdims=True)
    weights = jnp.sum(inv * part, axis=0, keepdims=True)
    t = inv + weights * (1.0 / math.sqrt(members - 1))
    t = t + (1.0 - jnp.sum(t, axis=1, keepdims=True)) * (1.0 / members)
    a, b = split(t)
    hi[...] = a
    lo[...] = b


def transform_of(gram):
    members = gram.shape[0]
    vmem = pl.BlockSpec(memory_space=pltpu.VMEM)
    return pl.pallas_call(
        functools.partial(factor_kernel, members),
        out_shape=[jax.ShapeDtypeStruct((members, members), jnp.bfloat16)] * 2,
        in_specs=[vmem],
        out_specs=[vmem] * 2,
        compiler_params=pltpu.CompilerParams(vmem_limit_bytes=12 * 2**20),
    )(gram)


def mix_kernel(members, hi, lo, fh, fu, fv, out):
    def mix(ref):
        dims = (((1,), (1,)), ((), ()))
        dot = functools.partial(lax.dot_general, dimension_numbers=dims, preferred_element_type=jnp.float32)
        rows = ref.shape[0]
        for r in range(rows):
            a, b = split(ref[r])
            out[0, pl.ds(r, members, stride=rows), :] = (
                dot(hi[...], a) + dot(hi[...], b) + dot(lo[...], a))

    for c, ref in enumerate((fh, fu, fv)):
        pl.when(pl.program_id(0) == c)(functools.partial(mix, ref))


def mixing(hi, lo, fields):
    rows, cols, members = fields[0].shape
    width = 128
    steps = cols // width

    def spec(c):
        return pl.BlockSpec((rows, width, members), lambda i, j: (0, jnp.where(i == c, j, jnp.where(i < c, 0, steps - 1)), 0))

    out = pl.pallas_call(
        functools.partial(mix_kernel, members),
        grid=(3, steps),
        out_shape=jax.ShapeDtypeStruct((3, members * rows, cols), jnp.float32),
        in_specs=[pl.BlockSpec((members, members), lambda i, j: (0, 0))] * 2 + [spec(c) for c in range(3)],
        out_specs=pl.BlockSpec((1, members * rows, width), lambda i, j: (i, 0, j)),
        compiler_params=pltpu.CompilerParams(vmem_limit_bytes=16 * 2**20),
    )(hi, lo, *fields)
    return out.reshape(3, members, rows, cols)


def shards(nlon, nlat, state, bathymetry, obs_index, obs_count, obs_value, obs_sd):
    h, u, v, part = forecast(nlon, nlat, state, bathymetry, obs_index, obs_count, obs_value, obs_sd)
    gram = total_sum(nlon, nlat, part)
    hi, lo = transform_of(gram)
    return mixing(hi, lo, (h, u, v))


def solution(mesh):
    return jax.shard_map(
        functools.partial(shards, mesh.shape["lon"], mesh.shape["lat"]),
        mesh=mesh,
        in_specs=(
            P(None, None, "lat", "lon"),
            P("lat", "lon"),
            P("lat", "lon", None),
            P("lat", "lon"),
            P("lat", "lon", None),
            P("lat", "lon", None),
        ),
        out_specs=P(None, None, "lat", "lon"),
        check_vma=False,
    )
```

```python
import functools
import math

import jax
import jax.numpy as jnp
from jax import lax
from jax.experimental import pallas as pl
from jax.experimental.pallas import tpu as pltpu
from jax.sharding import PartitionSpec as P

MESH = pl.DeviceIdType.MESH
PAD = 8


def forecast_kernel(nlon, nlat, members, rows, cols, state, bath_at, index_at, count_at, value_at, sd_at,
                    out_h, out_u, out_v, out, raw, hp, fu, fv, fxp, fy, brep, rbuf, csend, crecv, hx,
                    bath, index, count, value, sd, fc, part, other, acc, parts, whole, back,
                    lsem, isem, osem, rs, rr, cs, cr, ps, pr, ss, sr, gs, gr, qs, qr):
    lon, lat = lax.axis_index("lon"), lax.axis_index("lat")
    west, east = lax.rem(lon + nlon - 1, nlon), lax.rem(lon + 1, nlon)
    last = rows - 1
    has_n, has_s = lat > 0, lat < nlat - 1
    core, pair = lax.rem(lon, 2), lon // 2
    npair = nlon // 2
    peers = npair * nlat
    half = members // 2
    owners = min(peers, half // 8)
    chunk = half // owners
    me = lat * npair + pair
    partner = {"lon": lon + 1 - 2 * core}
    groups = members // 128
    tiles = cols // 128

    def device(p):
        return {"lon": 2 * lax.rem(p, npair) + core, "lat": p // npair}

    loads = [[pltpu.make_async_copy(state.at[c, :, pl.ds(128 * i, 128)], raw.at[c, i], lsem.at[c, i])
              for i in range(tiles)] for c in range(3)]
    small = [pltpu.make_async_copy(src, dst, isem.at[i]) for i, (src, dst) in enumerate((
        (bath_at, bath), (index_at, index), (count_at, count), (value_at, value), (sd_at, sd)))]
    small[0].start()
    for c in (2, 1, 0):
        for load in loads[c]:
            load.start()
    for load in small[1:]:
        load.start()
    barrier = pltpu.get_barrier_semaphore()
    pl.semaphore_signal(barrier, inc=1, device_id=partner, device_id_type=MESH)
    beyond = lax.rem(lon + nlon - 1 + 2 * core, nlon)
    pl.semaphore_signal(barrier, inc=1, device_id={"lon": beyond}, device_id_type=MESH)

    @pl.loop(1, peers)
    def _(d):
        pl.semaphore_signal(barrier, inc=1, device_id=device(lax.rem(me + d, peers)), device_id_type=MESH)

    small[0].wait()
    bt = bath[...].T
    for r in range(rows):
        brep[r] = jnp.broadcast_to(bt[:, r:r + 1], (cols, 128))
    at = (lat * rows + lax.broadcasted_iota(jnp.int32, (rows, 128), 0)).astype(jnp.float32)
    fc[...] = jnp.sin(math.pi / 3.0 * ((at + 0.5) / (rows * nlat) - 0.5))
    zero = jnp.zeros((cols, members), jnp.float32)

    @pl.when(jnp.logical_not(has_n))
    def _():
        for e in range(4):
            rbuf[e, 0] = zero

    @pl.when(jnp.logical_not(has_s))
    def _():
        for e in range(4):
            rbuf[e, 1] = zero

    def lanes(g):
        return pl.ds(128 * g, 128)

    def row_copy(e, g, north):
        if e % 2 == 0:
            src = fy.at[0 if north else last, :, lanes(g)]
        else:
            src = hp.at[0 if north else last, pl.ds(PAD, cols), lanes(g)]
        return pltpu.make_async_remote_copy(
            src_ref=src, dst_ref=rbuf.at[e, 1 if north else 0, :, lanes(g)],
            send_sem=rs.at[e, g, 0 if north else 1], recv_sem=rr.at[e, g, 1 if north else 0],
            device_id={"lat": lat - 1 if north else lat + 1}, device_id_type=MESH)

    def row_recv(e, g, side):
        here = rbuf.at[e, side, :, lanes(g)]
        return pltpu.make_async_remote_copy(
            src_ref=here, dst_ref=here, send_sem=rs.at[e, g, side], recv_sem=rr.at[e, g, side],
            device_id={"lat": lat - 1 if side == 0 else lat + 1}, device_id_type=MESH)

    def send_rows(e, g):
        @pl.when(has_n)
        def _():
            row_copy(e, g, True).start()

        @pl.when(has_s)
        def _():
            row_copy(e, g, False).start()

    def wait_rows(e, g):
        @pl.when(has_n)
        def _():
            row_copy(e, g, True).wait_send()
            row_recv(e, g, 0).wait_recv()

        @pl.when(has_s)
        def _():
            row_copy(e, g, False).wait_send()
            row_recv(e, g, 1).wait_recv()

    def col_copy(e, g, side):
        return pltpu.make_async_remote_copy(
            src_ref=csend.at[e, g, side], dst_ref=crecv.at[e, g, 1 - side],
            send_sem=cs.at[e, g, side], recv_sem=cr.at[e, g, 1 - side],
            device_id={"lon": west if side == 0 else east}, device_id_type=MESH)

    def send_cols(e, g, ref):
        for r in range(rows):
            csend[e, g, 0, r:r + 1, :] = ref[r, PAD:PAD + 1, lanes(g)]
            csend[e, g, 1, r:r + 1, :] = ref[r, PAD + cols - 1:PAD + cols, lanes(g)]
        col_copy(e, g, 0).start()
        col_copy(e, g, 1).start()

    def wait_cols(e, g, ref):
        for side in (0, 1):
            col_copy(e, g, side).wait()
        for r in range(rows):
            ref[r, PAD - 1:PAD, lanes(g)] = crecv[e, g, 0, r:r + 1, :]
            ref[r, PAD + cols:PAD + cols + 1, lanes(g)] = crecv[e, g, 1, r:r + 1, :]

    def slab(c, r, g):
        return jnp.concatenate(
            [raw[c, i, pl.ds(r + 128 * rows * g, 128, stride=rows), :].T for i in range(tiles)], axis=0)

    def dcol(ref, r, g):
        return ref[r, PAD + 1:PAD + cols + 1, lanes(g)] - ref[r, PAD - 1:PAD + cols - 1, lanes(g)]

    def hrow(r, g):
        return hp[r, PAD:PAD + cols, lanes(g)]

    def frow(r, g):
        return fy[r, :, lanes(g)]

    def load_v(r, g):
        v = slab(2, r, g)
        fv[r, :, lanes(g)] = v
        fy[r, :, lanes(g)] = v * brep[r]

    def height(r, g, up, down):
        div = dcol(fxp, r, g) + down - up
        hp[r, PAD:PAD + cols, lanes(g)] = hrow(r, g) - 0.25 * div

    def wind(r, g, up, down, flux):
        f = fc[pl.ds(r, 1), :]
        u, v = fu[r, :, lanes(g)], fv[r, :, lanes(g)]
        un = u + 0.5 * (f * v - 0.5 * dcol(hp, r, g))
        vn = v - 0.5 * (f * u + 0.5 * (down - up))
        fu[r, :, lanes(g)] = un
        fv[r, :, lanes(g)] = vn
        if flux:
            b = brep[r]
            fxp[r, PAD:PAD + cols, lanes(g)] = un * b
            fy[r, :, lanes(g)] = vn * b

    def edges_height(e, g):
        wait_rows(e, g)
        height(0, g, rbuf[e, 0, :, lanes(g)], frow(1, g))
        height(last, g, frow(last - 1, g), rbuf[e, 1, :, lanes(g)])
        send_rows(e + 1, g)

    def inner_height(g):
        @pl.loop(1, last)
        def _(r):
            height(r, g, frow(r - 1, g), frow(r + 1, g))

    def inner_wind(g, flux):
        @pl.loop(1, last)
        def _(r):
            wind(r, g, hrow(r - 1, g), hrow(r + 1, g), flux)

    def edges_wind(e, g, flux):
        wait_rows(e, g)
        wind(0, g, rbuf[e, 0, :, lanes(g)], hrow(1, g), flux)
        wind(last, g, hrow(last - 1, g), rbuf[e, 1, :, lanes(g)], flux)

    for load in loads[2]:
        load.wait()
    for g in range(groups):
        for r in (0, last):
            load_v(r, g)
        if g == 0:
            pl.semaphore_wait(barrier, peers + 1)
        send_rows(0, g)
    for load in loads[1]:
        load.wait()
    for g in range(groups):
        for r in range(rows):
            u = slab(1, r, g)
            fu[r, :, lanes(g)] = u
            fxp[r, PAD:PAD + cols, lanes(g)] = u * brep[r]
        send_cols(0, g, fxp)
        for r in range(1, last):
            load_v(r, g)
        if g == 0:
            for load in loads[0]:
                load.wait()
        for r in range(rows):
            hp[r, PAD:PAD + cols, lanes(g)] = slab(0, r, g)
        wait_cols(0, g, fxp)
        edges_height(0, g)
        inner_height(g)
        send_cols(1, g, hp)
    for g in range(groups):
        wait_cols(1, g, hp)
        inner_wind(g, True)
        edges_wind(1, g, True)
        send_rows(2, g)
        send_cols(2, g, fxp)
    for g in range(groups):
        wait_cols(2, g, fxp)
        inner_height(g)
        edges_height(2, g)
        send_cols(3, g, hp)

    out_copies = [
        pltpu.make_async_copy(hp.at[:, pl.ds(PAD, cols)], out_h, osem.at[0]),
        pltpu.make_async_copy(fu, out_u, osem.at[1]),
        pltpu.make_async_copy(fv, out_v, osem.at[2]),
    ]
    for load in small[1:]:
        load.wait()
    slots = hx.shape[0]

    @pl.loop(0, slots // 8)
    def _(t):
        got = []
        for k in range(8):
            cell = index[0, t * 8 + k]
            got.append(hp[cell // cols, pl.ds(PAD + lax.rem(cell, cols), 1), :])
        hx[pl.ds(t * 8, 8), :] = jnp.concatenate(got, axis=0)

    x = hx[...]
    info = jnp.concatenate([value[...], sd[...], jnp.zeros((6, slots), jnp.float32)], axis=0).T
    sigma = info[:, 1:2] * (math.sqrt(slots * nlon * nlat) / 16.0)
    valid = (lax.broadcasted_iota(jnp.int32, (slots, 1), 0) < count[0, 0]).astype(jnp.float32)
    mean = jnp.sum(x, axis=1, keepdims=True) * (1.0 / members)
    yp = (x - mean) * (valid / (math.sqrt(members - 1) * sigma))
    innov = (info[:, 0:1] - mean) * (valid / sigma)
    proj = jnp.sum(yp * innov, axis=0, keepdims=True)
    part[...] = jnp.dot(yp.T, yp, precision=lax.Precision.HIGHEST,
                        preferred_element_type=jnp.float32)
    part[members - 2:members - 1, 0:half] = proj[:, :half]
    part[members - 1:members, 0:half] = proj[:, half:]

    mine = pl.ds(pl.multiple_of(core * half, half), half)
    theirs = pl.ds(pl.multiple_of((1 - core) * half, half), half)

    def guard(cond, run):
        if owners == peers:
            run()
        else:
            pl.when(cond)(run)

    first = pltpu.make_async_remote_copy(
        src_ref=part.at[theirs], dst_ref=other, send_sem=ps, recv_sem=pr,
        device_id=partner, device_id_type=MESH)
    first.start()
    out_copies[0].start()
    first.wait()
    acc[...] = part[mine, :] + other[...]

    def scatter(p, frm):
        return pltpu.make_async_remote_copy(
            src_ref=acc.at[pl.ds(pl.multiple_of(p * chunk, chunk), chunk)], dst_ref=parts.at[frm],
            send_sem=ss.at[p], recv_sem=sr.at[frm], device_id=device(p), device_id_type=MESH)

    def arrive(frm):
        return pltpu.make_async_remote_copy(
            src_ref=parts.at[frm], dst_ref=parts.at[frm],
            send_sem=ss.at[0], recv_sem=sr.at[frm], device_id=device(frm), device_id_type=MESH)

    @pl.loop(1, peers)
    def _(d):
        p = lax.rem(me + d, peers)
        guard(p < owners, lambda: scatter(p, me).start())

    for g in range(groups):
        wait_cols(3, g, hp)
        inner_wind(g, False)

    def collect():
        total = acc[pl.ds(pl.multiple_of(me * chunk, chunk), chunk), :]

        def body(d, total):
            frm = lax.rem(me + d, peers)
            arrive(frm).wait_recv()
            return total + parts[frm]
        whole[me] = lax.fori_loop(1, peers, body, total)

    guard(me < owners, collect)

    def spread(p, frm):
        return pltpu.make_async_remote_copy(
            src_ref=whole.at[frm], dst_ref=whole.at[frm],
            send_sem=gs.at[p], recv_sem=gr.at[frm], device_id=device(p), device_id_type=MESH)

    def send_all():
        @pl.loop(1, peers)
        def _(d):
            p = lax.rem(me + d, peers)
            spread(p, me).start()

    guard(me < owners, send_all)
    for g in range(groups):
        edges_wind(3, g, False)
    out_copies[1].start()
    out_copies[2].start()

    @pl.loop(1, peers)
    def _(d):
        p = lax.rem(me + d, peers)
        guard(p < owners, lambda: spread(p, p).wait_recv())

    final = pltpu.make_async_remote_copy(
        src_ref=whole, dst_ref=back, send_sem=qs, recv_sem=qr,
        device_id=partner, device_id_type=MESH)
    final.start()

    @pl.loop(1, peers)
    def _(d):
        p = lax.rem(me + d, peers)
        guard(p < owners, lambda: scatter(p, me).wait_send())

    def sent_all():
        @pl.loop(1, peers)
        def _(d):
            p = lax.rem(me + d, peers)
            spread(p, me).wait_send()

    guard(me < owners, sent_all)
    out[mine, :] = whole[...].reshape(half, members)
    for copy in out_copies:
        copy.wait()
    final.wait()
    out[theirs, :] = back[...].reshape(half, members)


def forecast(nlon, nlat, state, bathymetry, obs_index, obs_count, obs_value, obs_sd):
    _, members, rows, cols = state.shape
    slots = obs_index.shape[2]
    f32, dma = jnp.float32, pltpu.SemaphoreType.DMA
    field = jax.ShapeDtypeStruct((rows, cols, members), f32)
    vmem, hbm = pl.BlockSpec(memory_space=pltpu.VMEM), pl.BlockSpec(memory_space=pltpu.HBM)
    half, peers, groups = members // 2, nlon // 2 * nlat, members // 128
    owners = min(peers, half // 8)
    chunk = half // owners
    return pl.pallas_call(
        functools.partial(forecast_kernel, nlon, nlat, members, rows, cols),
        out_shape=[field, field, field, jax.ShapeDtypeStruct((members, members), f32)],
        in_specs=[hbm] * 6,
        out_specs=[hbm] * 3 + [vmem],
        scratch_shapes=[
            pltpu.VMEM((3, cols // 128, members * rows, 128), f32),
            pltpu.VMEM((rows, cols + 2 * PAD, members), f32),
            pltpu.VMEM((rows, cols, members), f32),
            pltpu.VMEM((rows, cols, members), f32),
            pltpu.VMEM((rows, cols + 2 * PAD, members), f32),
            pltpu.VMEM((rows, cols, members), f32),
            pltpu.VMEM((rows, cols, 128), f32),
            pltpu.VMEM((4, 2, cols, members), f32),
            pltpu.VMEM((4, groups, 2, rows, 128), f32),
            pltpu.VMEM((4, groups, 2, rows, 128), f32),
            pltpu.VMEM((slots, members), f32),
            pltpu.VMEM((rows, cols), f32),
            pltpu.SMEM((1, slots), jnp.int32),
            pltpu.SMEM((1, 1), jnp.int32),
            pltpu.VMEM((1, slots), f32),
            pltpu.VMEM((1, slots), f32),
            pltpu.VMEM((rows, 128), f32),
            pltpu.VMEM((members, members), f32),
            pltpu.VMEM((half, members), f32), pltpu.VMEM((half, members), f32),
            pltpu.VMEM((peers, chunk, members), f32), pltpu.VMEM((owners, chunk, members), f32),
            pltpu.VMEM((owners, chunk, members), f32),
            dma((3, cols // 128)), dma((5,)), dma((3,)),
            dma((4, groups, 2)), dma((4, groups, 2)), dma((4, groups, 2)), dma((4, groups, 2)),
            dma, dma, dma((peers,)), dma((peers,)), dma((peers,)), dma((peers,)), dma, dma,
        ],
        compiler_params=pltpu.CompilerParams(
            collective_id=0, has_side_effects=True, vmem_limit_bytes=52 * 2**20),
    )(*(x if x.size == 1 else pltpu.with_memory_space_constraint(x, pltpu.HBM) for x in (
        state.reshape(3, members * rows, cols), bathymetry, obs_index.reshape(1, slots), obs_count,
        obs_value.reshape(1, slots), obs_sd.reshape(1, slots))))


def split(x):
    hi = x.astype(jnp.bfloat16)
    return hi, (x - hi.astype(jnp.float32)).astype(jnp.bfloat16)


def recip(x):
    r = pl.reciprocal(x, approx=True)
    return r * (2.0 - x * r)


def tree_sum(terms):
    while len(terms) > 1:
        terms = [sum(terms[i:i + 2][1:], terms[i]) for i in range(0, len(terms), 2)]
    return terms[0]


def invert_block(x):
    size, step = x.shape[0], 16
    lane = lax.broadcasted_iota(jnp.int32, (step, size), 1)
    sub = lax.broadcasted_iota(jnp.int32, (step, size), 0)
    blocks = [x[i:i + step, :] for i in range(0, size, step)]
    done = []
    for t in range(size // step):
        base = step * t
        row = blocks[t]
        inpanel = (lane >= base) & (lane < base + step)
        diag = [jnp.broadcast_to(row[:, base + q:base + q + 1], (step, size)) for q in range(step)]
        aug = jnp.where(inpanel, jnp.where(lane == base + sub, 1.0, 0.0), row)
        inv = jnp.zeros((step, size), jnp.float32)
        piv = jnp.ones((step, size), jnp.float32)
        for k in range(0, step, 2):
            d0, d1 = diag[k], diag[k + 1]
            a, b, c = d0[k:k + 1, :], d1[k:k + 1, :], d1[k + 1:k + 2, :]
            det = a * c - b * b
            ra, rdet = recip(a), recip(det)
            ratio, rp = b * ra, a * rdet
            inv = jnp.where(sub == k, ra, jnp.where(sub == k + 1, rp, inv))
            piv = jnp.where(sub == k, a, jnp.where(sub == k + 1, det * ra, piv))
            l0 = jnp.where(sub > k, d0 * ra, 0.0)
            l1 = jnp.where(sub > k + 1, (d1 - l0 * b) * rp, 0.0)

            def eliminate(z):
                first = z[k:k + 1, :]
                second = z[k + 1:k + 2, :] - ratio * first
                return z - (l0 * first + l1 * second)

            for q in range(k + 2, step):
                diag[q] = eliminate(diag[q])
            aug = eliminate(aug)
        done.append(jnp.where(lane < base + step, aug, 0.0) * lax.rsqrt(piv))
        if base + step < size:
            factor = (aug * inv).T
            for s in range(t + 1, size // step):
                fac = factor[step * s:step * (s + 1), :]
                terms = [fac[:, k:k + 1] * aug[k:k + 1, :] for k in range(step)]
                blocks[s] = jnp.where(inpanel, 0.0, blocks[s]) - tree_sum(terms)
    return jnp.concatenate(done, axis=0)


def dot_at(x, y, dims):
    return lax.dot_general(x, y, (dims, ((), ())), precision=lax.Precision.HIGHEST,
                           preferred_element_type=jnp.float32)


def invert(gram):
    size = gram.shape[0]
    half = size // 2
    i = lax.broadcasted_iota(jnp.int32, (half, half), 0)
    j = lax.broadcasted_iota(jnp.int32, (half, half), 1)
    eye = (i == j).astype(jnp.float32)
    m1 = invert_block(gram[:half, :half] + eye)
    side = dot_at(m1, gram[:half, half:], ((1,), (0,)))
    st = side.T
    m2 = invert_block(gram[half:, half:] + eye - dot_at(st, side, ((1,), (0,))))
    low = -dot_at(m2, dot_at(st, m1, ((1,), (0,))), ((1,), (0,)))
    top = jnp.concatenate([m1, jnp.zeros((half, half), jnp.float32)], axis=1)
    return jnp.concatenate([top, jnp.concatenate([low, m2], axis=1)], axis=0)


def factor_kernel(members, gram, hi, lo):
    g = gram[...]
    half = members // 2
    proj = jnp.concatenate([g[members - 2:members - 1, :half], g[members - 1:members, :half]], axis=1)
    inv = invert(g)
    part = jnp.sum(inv * proj, axis=1, keepdims=True)
    weights = jnp.sum(inv * part, axis=0, keepdims=True)
    t = inv + weights * (1.0 / math.sqrt(members - 1))
    t = t + (1.0 - jnp.sum(t, axis=1, keepdims=True)) * (1.0 / members)
    a, b = split(t)
    hi[...] = a
    lo[...] = b


def transform_of(gram):
    members = gram.shape[0]
    vmem = pl.BlockSpec(memory_space=pltpu.VMEM)
    return pl.pallas_call(
        functools.partial(factor_kernel, members),
        out_shape=[jax.ShapeDtypeStruct((members, members), jnp.bfloat16)] * 2,
        in_specs=[vmem],
        out_specs=[vmem] * 2,
        compiler_params=pltpu.CompilerParams(vmem_limit_bytes=12 * 2**20),
    )(gram)


def mix_kernel(members, hi, lo, fh, fu, fv, out):
    def mix(ref):
        dims = (((1,), (1,)), ((), ()))
        dot = functools.partial(lax.dot_general, dimension_numbers=dims, preferred_element_type=jnp.float32)
        rows = ref.shape[0]
        for r in range(rows):
            a, b = split(ref[r])
            out[0, pl.ds(r, members, stride=rows), :] = (
                dot(hi[...], a) + dot(hi[...], b) + dot(lo[...], a))

    for c, ref in enumerate((fh, fu, fv)):
        pl.when(pl.program_id(0) == c)(functools.partial(mix, ref))


def mixing(hi, lo, fields):
    rows, cols, members = fields[0].shape
    width = 128
    steps = cols // width

    def spec(c):
        return pl.BlockSpec((rows, width, members), lambda i, j: (0, jnp.where(i == c, j, jnp.where(i < c, 0, steps - 1)), 0))

    out = pl.pallas_call(
        functools.partial(mix_kernel, members),
        grid=(3, steps),
        out_shape=jax.ShapeDtypeStruct((3, members * rows, cols), jnp.float32),
        in_specs=[pl.BlockSpec((members, members), lambda i, j: (0, 0))] * 2 + [spec(c) for c in range(3)],
        out_specs=pl.BlockSpec((1, members * rows, width), lambda i, j: (i, 0, j)),
        compiler_params=pltpu.CompilerParams(vmem_limit_bytes=16 * 2**20),
    )(hi, lo, *fields)
    return out.reshape(3, members, rows, cols)


def shards(nlon, nlat, state, bathymetry, obs_index, obs_count, obs_value, obs_sd):
    h, u, v, gram = forecast(nlon, nlat, state, bathymetry, obs_index, obs_count, obs_value, obs_sd)
    h, u, v = (pltpu.with_memory_space_constraint(x, pltpu.HBM) for x in (h, u, v))
    hi, lo = transform_of(gram)
    return mixing(hi, lo, (h, u, v))


def solution(mesh):
    return jax.shard_map(
        functools.partial(shards, mesh.shape["lon"], mesh.shape["lat"]),
        mesh=mesh,
        in_specs=(
            P(None, None, "lat", "lon"),
            P("lat", "lon"),
            P("lat", "lon", None),
            P("lat", "lon"),
            P("lat", "lon", None),
            P("lat", "lon", None),
        ),
        out_specs=P(None, None, "lat", "lon"),
        check_vma=False,
    )
```

```python
import functools
import math

import jax
import jax.numpy as jnp
from jax import lax
from jax.experimental import pallas as pl
from jax.experimental.pallas import tpu as pltpu
from jax.sharding import PartitionSpec as P

MESH = pl.DeviceIdType.MESH
PAD = 8


def forecast_kernel(nlon, nlat, members, rows, cols, state, bath_at, index_at, count_at, value_at, sd_at,
                    hp, fu, fv, out, raw, fxp, fy, brep, rbuf, csend, crecv, hx,
                    bath, index, count, value, sd, fc, part, other, acc, parts, whole, back,
                    lsem, isem, rs, rr, cs, cr, ps, pr, ss, sr, gs, gr, qs, qr):
    lon, lat = lax.axis_index("lon"), lax.axis_index("lat")
    west, east = lax.rem(lon + nlon - 1, nlon), lax.rem(lon + 1, nlon)
    last = rows - 1
    has_n, has_s = lat > 0, lat < nlat - 1
    core, pair = lax.rem(lon, 2), lon // 2
    npair = nlon // 2
    peers = npair * nlat
    half = members // 2
    owners = min(peers, half // 8)
    chunk = half // owners
    me = lat * npair + pair
    partner = {"lon": lon + 1 - 2 * core}
    groups = members // 128
    tiles = cols // 128

    def device(p):
        return {"lon": 2 * lax.rem(p, npair) + core, "lat": p // npair}

    loads = [[pltpu.make_async_copy(state.at[c, :, pl.ds(128 * i, 128)], raw.at[c, i], lsem.at[c, i])
              for i in range(tiles)] for c in range(3)]
    small = [pltpu.make_async_copy(src, dst, isem.at[i]) for i, (src, dst) in enumerate((
        (bath_at, bath), (index_at, index), (count_at, count), (value_at, value), (sd_at, sd)))]
    small[0].start()
    for c in (2, 1, 0):
        for load in loads[c]:
            load.start()
    for load in small[1:]:
        load.start()
    barrier = pltpu.get_barrier_semaphore()
    pl.semaphore_signal(barrier, inc=1, device_id=partner, device_id_type=MESH)
    beyond = lax.rem(lon + nlon - 1 + 2 * core, nlon)
    pl.semaphore_signal(barrier, inc=1, device_id={"lon": beyond}, device_id_type=MESH)

    @pl.loop(1, peers)
    def _(d):
        pl.semaphore_signal(barrier, inc=1, device_id=device(lax.rem(me + d, peers)), device_id_type=MESH)

    small[0].wait()
    bt = bath[...].T
    for r in range(rows):
        brep[r] = jnp.broadcast_to(bt[:, r:r + 1], (cols, 128))
    at = (lat * rows + lax.broadcasted_iota(jnp.int32, (rows, 128), 0)).astype(jnp.float32)
    fc[...] = jnp.sin(math.pi / 3.0 * ((at + 0.5) / (rows * nlat) - 0.5))
    zero = jnp.zeros((cols, members), jnp.float32)

    @pl.when(jnp.logical_not(has_n))
    def _():
        for e in range(4):
            rbuf[e, 0] = zero

    @pl.when(jnp.logical_not(has_s))
    def _():
        for e in range(4):
            rbuf[e, 1] = zero

    def lanes(g):
        return pl.ds(128 * g, 128)

    def row_copy(e, g, north):
        if e % 2 == 0:
            src = fy.at[0 if north else last, :, lanes(g)]
        else:
            src = hp.at[0 if north else last, pl.ds(PAD, cols), lanes(g)]
        return pltpu.make_async_remote_copy(
            src_ref=src, dst_ref=rbuf.at[e, 1 if north else 0, :, lanes(g)],
            send_sem=rs.at[e, g, 0 if north else 1], recv_sem=rr.at[e, g, 1 if north else 0],
            device_id={"lat": lat - 1 if north else lat + 1}, device_id_type=MESH)

    def row_recv(e, g, side):
        here = rbuf.at[e, side, :, lanes(g)]
        return pltpu.make_async_remote_copy(
            src_ref=here, dst_ref=here, send_sem=rs.at[e, g, side], recv_sem=rr.at[e, g, side],
            device_id={"lat": lat - 1 if side == 0 else lat + 1}, device_id_type=MESH)

    def send_rows(e, g):
        @pl.when(has_n)
        def _():
            row_copy(e, g, True).start()

        @pl.when(has_s)
        def _():
            row_copy(e, g, False).start()

    def wait_rows(e, g):
        @pl.when(has_n)
        def _():
            row_copy(e, g, True).wait_send()
            row_recv(e, g, 0).wait_recv()

        @pl.when(has_s)
        def _():
            row_copy(e, g, False).wait_send()
            row_recv(e, g, 1).wait_recv()

    def col_copy(e, g, side):
        return pltpu.make_async_remote_copy(
            src_ref=csend.at[e, g, side], dst_ref=crecv.at[e, g, 1 - side],
            send_sem=cs.at[e, g, side], recv_sem=cr.at[e, g, 1 - side],
            device_id={"lon": west if side == 0 else east}, device_id_type=MESH)

    def send_cols(e, g, ref):
        for r in range(rows):
            csend[e, g, 0, r:r + 1, :] = ref[r, PAD:PAD + 1, lanes(g)]
            csend[e, g, 1, r:r + 1, :] = ref[r, PAD + cols - 1:PAD + cols, lanes(g)]
        col_copy(e, g, 0).start()
        col_copy(e, g, 1).start()

    def wait_cols(e, g, ref):
        for side in (0, 1):
            col_copy(e, g, side).wait()
        for r in range(rows):
            ref[r, PAD - 1:PAD, lanes(g)] = crecv[e, g, 0, r:r + 1, :]
            ref[r, PAD + cols:PAD + cols + 1, lanes(g)] = crecv[e, g, 1, r:r + 1, :]

    def slab(c, r, g):
        return jnp.concatenate(
            [raw[c, i, pl.ds(r + 128 * rows * g, 128, stride=rows), :].T for i in range(tiles)], axis=0)

    def dcol(ref, r, g):
        return ref[r, PAD + 1:PAD + cols + 1, lanes(g)] - ref[r, PAD - 1:PAD + cols - 1, lanes(g)]

    def hrow(r, g):
        return hp[r, PAD:PAD + cols, lanes(g)]

    def frow(r, g):
        return fy[r, :, lanes(g)]

    def load_v(r, g):
        v = slab(2, r, g)
        fv[r, :, lanes(g)] = v
        fy[r, :, lanes(g)] = v * brep[r]

    def height(r, g, up, down):
        div = dcol(fxp, r, g) + down - up
        hp[r, PAD:PAD + cols, lanes(g)] = hrow(r, g) - 0.25 * div

    def wind(r, g, up, down, flux):
        f = fc[pl.ds(r, 1), :]
        u, v = fu[r, :, lanes(g)], fv[r, :, lanes(g)]
        un = u + 0.5 * (f * v - 0.5 * dcol(hp, r, g))
        vn = v - 0.5 * (f * u + 0.5 * (down - up))
        fu[r, :, lanes(g)] = un
        fv[r, :, lanes(g)] = vn
        if flux:
            b = brep[r]
            fxp[r, PAD:PAD + cols, lanes(g)] = un * b
            fy[r, :, lanes(g)] = vn * b

    def edges_height(e, g):
        wait_rows(e, g)
        height(0, g, rbuf[e, 0, :, lanes(g)], frow(1, g))
        height(last, g, frow(last - 1, g), rbuf[e, 1, :, lanes(g)])
        send_rows(e + 1, g)

    def inner_height(g):
        @pl.loop(1, last)
        def _(r):
            height(r, g, frow(r - 1, g), frow(r + 1, g))

    def inner_wind(g, flux):
        @pl.loop(1, last)
        def _(r):
            wind(r, g, hrow(r - 1, g), hrow(r + 1, g), flux)

    def edges_wind(e, g, flux):
        wait_rows(e, g)
        wind(0, g, rbuf[e, 0, :, lanes(g)], hrow(1, g), flux)
        wind(last, g, hrow(last - 1, g), rbuf[e, 1, :, lanes(g)], flux)

    for load in loads[2]:
        load.wait()
    for g in range(groups):
        for r in (0, last):
            load_v(r, g)
        if g == 0:
            pl.semaphore_wait(barrier, peers + 1)
        send_rows(0, g)
    for load in loads[1]:
        load.wait()
    for g in range(groups):
        for r in range(rows):
            u = slab(1, r, g)
            fu[r, :, lanes(g)] = u
            fxp[r, PAD:PAD + cols, lanes(g)] = u * brep[r]
        send_cols(0, g, fxp)
        for r in range(1, last):
            load_v(r, g)
        if g == 0:
            for load in loads[0]:
                load.wait()
        for r in range(rows):
            hp[r, PAD:PAD + cols, lanes(g)] = slab(0, r, g)
        wait_cols(0, g, fxp)
        edges_height(0, g)
        inner_height(g)
        send_cols(1, g, hp)
    for g in range(groups):
        wait_cols(1, g, hp)
        inner_wind(g, True)
        edges_wind(1, g, True)
        send_rows(2, g)
        send_cols(2, g, fxp)
    for g in range(groups):
        wait_cols(2, g, fxp)
        inner_height(g)
        edges_height(2, g)
        send_cols(3, g, hp)

    for load in small[1:]:
        load.wait()
    slots = hx.shape[0]

    @pl.loop(0, slots // 8)
    def _(t):
        got = []
        for k in range(8):
            cell = index[0, t * 8 + k]
            got.append(hp[cell // cols, pl.ds(PAD + lax.rem(cell, cols), 1), :])
        hx[pl.ds(t * 8, 8), :] = jnp.concatenate(got, axis=0)

    x = hx[...]
    info = jnp.concatenate([value[...], sd[...], jnp.zeros((6, slots), jnp.float32)], axis=0).T
    sigma = info[:, 1:2] * (math.sqrt(slots * nlon * nlat) / 16.0)
    valid = (lax.broadcasted_iota(jnp.int32, (slots, 1), 0) < count[0, 0]).astype(jnp.float32)
    mean = jnp.sum(x, axis=1, keepdims=True) * (1.0 / members)
    yp = (x - mean) * (valid / (math.sqrt(members - 1) * sigma))
    innov = (info[:, 0:1] - mean) * (valid / sigma)
    proj = jnp.sum(yp * innov, axis=0, keepdims=True)
    part[...] = jnp.dot(yp.T, yp, precision=lax.Precision.HIGHEST,
                        preferred_element_type=jnp.float32)
    part[members - 2:members - 1, 0:half] = proj[:, :half]
    part[members - 1:members, 0:half] = proj[:, half:]

    mine = pl.ds(pl.multiple_of(core * half, half), half)
    theirs = pl.ds(pl.multiple_of((1 - core) * half, half), half)

    def guard(cond, run):
        if owners == peers:
            run()
        else:
            pl.when(cond)(run)

    first = pltpu.make_async_remote_copy(
        src_ref=part.at[theirs], dst_ref=other, send_sem=ps, recv_sem=pr,
        device_id=partner, device_id_type=MESH)
    first.start()
    first.wait()
    acc[...] = part[mine, :] + other[...]

    def scatter(p, frm):
        return pltpu.make_async_remote_copy(
            src_ref=acc.at[pl.ds(pl.multiple_of(p * chunk, chunk), chunk)], dst_ref=parts.at[frm],
            send_sem=ss.at[p], recv_sem=sr.at[frm], device_id=device(p), device_id_type=MESH)

    def arrive(frm):
        return pltpu.make_async_remote_copy(
            src_ref=parts.at[frm], dst_ref=parts.at[frm],
            send_sem=ss.at[0], recv_sem=sr.at[frm], device_id=device(frm), device_id_type=MESH)

    @pl.loop(1, peers)
    def _(d):
        p = lax.rem(me + d, peers)
        guard(p < owners, lambda: scatter(p, me).start())

    for g in range(groups):
        wait_cols(3, g, hp)
        inner_wind(g, False)

    def collect():
        total = acc[pl.ds(pl.multiple_of(me * chunk, chunk), chunk), :]

        def body(d, total):
            frm = lax.rem(me + d, peers)
            arrive(frm).wait_recv()
            return total + parts[frm]
        whole[me] = lax.fori_loop(1, peers, body, total)

    guard(me < owners, collect)

    def spread(p, frm):
        return pltpu.make_async_remote_copy(
            src_ref=whole.at[frm], dst_ref=whole.at[frm],
            send_sem=gs.at[p], recv_sem=gr.at[frm], device_id=device(p), device_id_type=MESH)

    def send_all():
        @pl.loop(1, peers)
        def _(d):
            p = lax.rem(me + d, peers)
            spread(p, me).start()

    guard(me < owners, send_all)
    for g in range(groups):
        edges_wind(3, g, False)

    @pl.loop(1, peers)
    def _(d):
        p = lax.rem(me + d, peers)
        guard(p < owners, lambda: spread(p, p).wait_recv())

    final = pltpu.make_async_remote_copy(
        src_ref=whole, dst_ref=back, send_sem=qs, recv_sem=qr,
        device_id=partner, device_id_type=MESH)
    final.start()

    @pl.loop(1, peers)
    def _(d):
        p = lax.rem(me + d, peers)
        guard(p < owners, lambda: scatter(p, me).wait_send())

    def sent_all():
        @pl.loop(1, peers)
        def _(d):
            p = lax.rem(me + d, peers)
            spread(p, me).wait_send()

    guard(me < owners, sent_all)
    out[mine, :] = whole[...].reshape(half, members)
    final.wait()
    out[theirs, :] = back[...].reshape(half, members)


def forecast(nlon, nlat, state, bathymetry, obs_index, obs_count, obs_value, obs_sd):
    _, members, rows, cols = state.shape
    slots = obs_index.shape[2]
    f32, dma = jnp.float32, pltpu.SemaphoreType.DMA
    field = jax.ShapeDtypeStruct((rows, cols, members), f32)
    vmem, hbm = pl.BlockSpec(memory_space=pltpu.VMEM), pl.BlockSpec(memory_space=pltpu.HBM)
    half, peers, groups = members // 2, nlon // 2 * nlat, members // 128
    owners = min(peers, half // 8)
    chunk = half // owners
    return pl.pallas_call(
        functools.partial(forecast_kernel, nlon, nlat, members, rows, cols),
        out_shape=[jax.ShapeDtypeStruct((rows, cols + 2 * PAD, members), f32), field, field, jax.ShapeDtypeStruct((members, members), f32)],
        in_specs=[hbm] * 6,
        out_specs=[vmem] * 4,
        scratch_shapes=[
            pltpu.VMEM((3, cols // 128, members * rows, 128), f32),
            pltpu.VMEM((rows, cols + 2 * PAD, members), f32),
            pltpu.VMEM((rows, cols, members), f32),
            pltpu.VMEM((rows, cols, 128), f32),
            pltpu.VMEM((4, 2, cols, members), f32),
            pltpu.VMEM((4, groups, 2, rows, 128), f32),
            pltpu.VMEM((4, groups, 2, rows, 128), f32),
            pltpu.VMEM((slots, members), f32),
            pltpu.VMEM((rows, cols), f32),
            pltpu.SMEM((1, slots), jnp.int32),
            pltpu.SMEM((1, 1), jnp.int32),
            pltpu.VMEM((1, slots), f32),
            pltpu.VMEM((1, slots), f32),
            pltpu.VMEM((rows, 128), f32),
            pltpu.VMEM((members, members), f32),
            pltpu.VMEM((half, members), f32), pltpu.VMEM((half, members), f32),
            pltpu.VMEM((peers, chunk, members), f32), pltpu.VMEM((owners, chunk, members), f32),
            pltpu.VMEM((owners, chunk, members), f32),
            dma((3, cols // 128)), dma((5,)),
            dma((4, groups, 2)), dma((4, groups, 2)), dma((4, groups, 2)), dma((4, groups, 2)),
            dma, dma, dma((peers,)), dma((peers,)), dma((peers,)), dma((peers,)), dma, dma,
        ],
        compiler_params=pltpu.CompilerParams(
            collective_id=0, has_side_effects=True, vmem_limit_bytes=30 * 2**20),
    )(*(x if x.size == 1 else pltpu.with_memory_space_constraint(x, pltpu.HBM) for x in (
        state.reshape(3, members * rows, cols), bathymetry, obs_index.reshape(1, slots), obs_count,
        obs_value.reshape(1, slots), obs_sd.reshape(1, slots))))


def split(x):
    hi = x.astype(jnp.bfloat16)
    return hi, (x - hi.astype(jnp.float32)).astype(jnp.bfloat16)


def recip(x):
    r = pl.reciprocal(x, approx=True)
    return r * (2.0 - x * r)


def tree_sum(terms):
    while len(terms) > 1:
        terms = [sum(terms[i:i + 2][1:], terms[i]) for i in range(0, len(terms), 2)]
    return terms[0]


def invert_block(x):
    size, step = x.shape[0], 16
    lane = lax.broadcasted_iota(jnp.int32, (step, size), 1)
    sub = lax.broadcasted_iota(jnp.int32, (step, size), 0)
    blocks = [x[i:i + step, :] for i in range(0, size, step)]
    done = []
    for t in range(size // step):
        base = step * t
        row = blocks[t]
        inpanel = (lane >= base) & (lane < base + step)
        diag = [jnp.broadcast_to(row[:, base + q:base + q + 1], (step, size)) for q in range(step)]
        aug = jnp.where(inpanel, jnp.where(lane == base + sub, 1.0, 0.0), row)
        inv = jnp.zeros((step, size), jnp.float32)
        piv = jnp.ones((step, size), jnp.float32)
        for k in range(0, step, 2):
            d0, d1 = diag[k], diag[k + 1]
            a, b, c = d0[k:k + 1, :], d1[k:k + 1, :], d1[k + 1:k + 2, :]
            det = a * c - b * b
            ra, rdet = recip(a), recip(det)
            ratio, rp = b * ra, a * rdet
            inv = jnp.where(sub == k, ra, jnp.where(sub == k + 1, rp, inv))
            piv = jnp.where(sub == k, a, jnp.where(sub == k + 1, det * ra, piv))
            l0 = jnp.where(sub > k, d0 * ra, 0.0)
            l1 = jnp.where(sub > k + 1, (d1 - l0 * b) * rp, 0.0)

            def eliminate(z):
                first = z[k:k + 1, :]
                second = z[k + 1:k + 2, :] - ratio * first
                return z - (l0 * first + l1 * second)

            for q in range(k + 2, step):
                diag[q] = eliminate(diag[q])
            aug = eliminate(aug)
        done.append(jnp.where(lane < base + step, aug, 0.0) * lax.rsqrt(piv))
        if base + step < size:
            factor = (aug * inv).T
            for s in range(t + 1, size // step):
                fac = factor[step * s:step * (s + 1), :]
                terms = [fac[:, k:k + 1] * aug[k:k + 1, :] for k in range(step)]
                blocks[s] = jnp.where(inpanel, 0.0, blocks[s]) - tree_sum(terms)
    return jnp.concatenate(done, axis=0)


def dot_at(x, y, dims):
    return lax.dot_general(x, y, (dims, ((), ())), precision=lax.Precision.HIGHEST,
                           preferred_element_type=jnp.float32)


def invert(gram):
    size = gram.shape[0]
    half = size // 2
    i = lax.broadcasted_iota(jnp.int32, (half, half), 0)
    j = lax.broadcasted_iota(jnp.int32, (half, half), 1)
    eye = (i == j).astype(jnp.float32)
    m1 = invert_block(gram[:half, :half] + eye)
    side = dot_at(m1, gram[:half, half:], ((1,), (0,)))
    st = side.T
    m2 = invert_block(gram[half:, half:] + eye - dot_at(st, side, ((1,), (0,))))
    low = -dot_at(m2, dot_at(st, m1, ((1,), (0,))), ((1,), (0,)))
    top = jnp.concatenate([m1, jnp.zeros((half, half), jnp.float32)], axis=1)
    return jnp.concatenate([top, jnp.concatenate([low, m2], axis=1)], axis=0)


def analysis_kernel(members, gram, hp, fu, fv, out, hi, lo, buf, sem):
    g = gram[...]
    half = members // 2
    proj = jnp.concatenate([g[members - 2:members - 1, :half], g[members - 1:members, :half]], axis=1)
    inv = invert(g)
    part = jnp.sum(inv * proj, axis=1, keepdims=True)
    weights = jnp.sum(inv * part, axis=0, keepdims=True)
    t = inv + weights * (1.0 / math.sqrt(members - 1))
    t = t + (1.0 - jnp.sum(t, axis=1, keepdims=True)) * (1.0 / members)
    a, b = split(t)
    hi[...] = a
    lo[...] = b
    dims = (((1,), (1,)), ((), ()))
    dot = functools.partial(lax.dot_general, dimension_numbers=dims, preferred_element_type=jnp.float32)
    rows, cols, _ = fu.shape
    copies = []
    for c, ref in enumerate((hp, fu, fv)):
        skip = PAD if c == 0 else 0
        for i in range(cols // 128):
            for r in range(0, rows, 2):
                x = jnp.concatenate(
                    [ref[r + k, skip + 128 * i:skip + 128 * (i + 1), :] for k in range(2)], axis=0)
                a, b = split(x)
                mixed = dot(hi[...], a) + dot(hi[...], b) + dot(lo[...], a)
                for k in range(2):
                    buf[c, i, pl.ds(r + k, members, stride=rows), :] = mixed[:, 128 * k:128 * (k + 1)]
            copy = pltpu.make_async_copy(buf.at[c, i], out.at[c, :, pl.ds(128 * i, 128)], sem.at[c, i])
            copy.start()
            copies.append(copy)
    for copy in copies:
        copy.wait()


def analyse(gram, fields):
    rows, cols, members = fields[1].shape
    tiles = cols // 128
    vmem = pl.BlockSpec(memory_space=pltpu.VMEM)
    out = pl.pallas_call(
        functools.partial(analysis_kernel, members),
        out_shape=jax.ShapeDtypeStruct((3, members * rows, cols), jnp.float32),
        in_specs=[vmem] * 4,
        out_specs=pl.BlockSpec(memory_space=pltpu.HBM),
        scratch_shapes=[pltpu.VMEM((members, members), jnp.bfloat16)] * 2 + [
            pltpu.VMEM((3, tiles, members * rows, 128), jnp.float32),
            pltpu.SemaphoreType.DMA((3, tiles))],
        compiler_params=pltpu.CompilerParams(vmem_limit_bytes=20 * 2**20),
    )(gram, *fields)
    return out.reshape(3, members, rows, cols)


def shards(nlon, nlat, state, bathymetry, obs_index, obs_count, obs_value, obs_sd):
    h, u, v, gram = forecast(nlon, nlat, state, bathymetry, obs_index, obs_count, obs_value, obs_sd)
    return analyse(gram, (h, u, v))


def solution(mesh):
    return jax.shard_map(
        functools.partial(shards, mesh.shape["lon"], mesh.shape["lat"]),
        mesh=mesh,
        in_specs=(
            P(None, None, "lat", "lon"),
            P("lat", "lon"),
            P("lat", "lon", None),
            P("lat", "lon"),
            P("lat", "lon", None),
            P("lat", "lon", None),
        ),
        out_specs=P(None, None, "lat", "lon"),
        check_vma=False,
    )
```

```python
import functools
import math

import jax
import jax.numpy as jnp
from jax import lax
from jax.experimental import pallas as pl
from jax.experimental.pallas import tpu as pltpu
from jax.sharding import PartitionSpec as P

MESH = pl.DeviceIdType.MESH
PAD = 8


def forecast_kernel(nlon, nlat, members, rows, cols, state, bath_at, index_at, count_at, value_at, sd_at,
                    hp, fu, fv, out, raw, fxp, fy, brep, rbuf, csend, crecv, hx,
                    bath, index, count, value, sd, fc, yt, part, other, acc, parts, whole, back,
                    lsem, isem, rs, rr, cs, cr, ps, pr, ss, sr, gs, gr, qs, qr):
    lon, lat = lax.axis_index("lon"), lax.axis_index("lat")
    west, east = lax.rem(lon + nlon - 1, nlon), lax.rem(lon + 1, nlon)
    last = rows - 1
    has_n, has_s = lat > 0, lat < nlat - 1
    core, pair = lax.rem(lon, 2), lon // 2
    npair = nlon // 2
    peers = npair * nlat
    half = members // 2
    owners = min(peers, half // 8)
    chunk = half // owners
    me = lat * npair + pair
    partner = {"lon": lon + 1 - 2 * core}
    groups = members // 128
    tiles = cols // 128

    def device(p):
        return {"lon": 2 * lax.rem(p, npair) + core, "lat": p // npair}

    loads = [[pltpu.make_async_copy(state.at[c, :, pl.ds(128 * i, 128)], raw.at[c, i], lsem.at[c, i])
              for i in range(tiles)] for c in range(3)]
    small = [pltpu.make_async_copy(src, dst, isem.at[i]) for i, (src, dst) in enumerate((
        (bath_at, bath), (index_at, index), (count_at, count), (value_at, value), (sd_at, sd)))]
    small[0].start()
    for c in (2, 1, 0):
        for load in loads[c]:
            load.start()
    for load in small[1:]:
        load.start()
    barrier = pltpu.get_barrier_semaphore()
    pl.semaphore_signal(barrier, inc=1, device_id=partner, device_id_type=MESH)
    beyond = lax.rem(lon + nlon - 1 + 2 * core, nlon)
    pl.semaphore_signal(barrier, inc=1, device_id={"lon": beyond}, device_id_type=MESH)

    @pl.loop(1, peers)
    def _(d):
        pl.semaphore_signal(barrier, inc=1, device_id=device(lax.rem(me + d, peers)), device_id_type=MESH)

    small[0].wait()
    bt = bath[...].T
    for r in range(rows):
        brep[r] = jnp.broadcast_to(bt[:, r:r + 1], (cols, 128))
    at = (lat * rows + lax.broadcasted_iota(jnp.int32, (rows, 128), 0)).astype(jnp.float32)
    fc[...] = jnp.sin(math.pi / 3.0 * ((at + 0.5) / (rows * nlat) - 0.5))
    zero = jnp.zeros((cols, members), jnp.float32)

    @pl.when(jnp.logical_not(has_n))
    def _():
        for e in range(4):
            rbuf[e, 0] = zero

    @pl.when(jnp.logical_not(has_s))
    def _():
        for e in range(4):
            rbuf[e, 1] = zero

    def lanes(g):
        return pl.ds(128 * g, 128)

    def row_copy(e, g, north):
        if e % 2 == 0:
            src = fy.at[0 if north else last, :, lanes(g)]
        else:
            src = hp.at[0 if north else last, pl.ds(PAD, cols), lanes(g)]
        return pltpu.make_async_remote_copy(
            src_ref=src, dst_ref=rbuf.at[e, 1 if north else 0, :, lanes(g)],
            send_sem=rs.at[e, g, 0 if north else 1], recv_sem=rr.at[e, g, 1 if north else 0],
            device_id={"lat": lat - 1 if north else lat + 1}, device_id_type=MESH)

    def row_recv(e, g, side):
        here = rbuf.at[e, side, :, lanes(g)]
        return pltpu.make_async_remote_copy(
            src_ref=here, dst_ref=here, send_sem=rs.at[e, g, side], recv_sem=rr.at[e, g, side],
            device_id={"lat": lat - 1 if side == 0 else lat + 1}, device_id_type=MESH)

    def send_rows(e, g):
        @pl.when(has_n)
        def _():
            row_copy(e, g, True).start()

        @pl.when(has_s)
        def _():
            row_copy(e, g, False).start()

    def wait_rows(e, g):
        @pl.when(has_n)
        def _():
            row_copy(e, g, True).wait_send()
            row_recv(e, g, 0).wait_recv()

        @pl.when(has_s)
        def _():
            row_copy(e, g, False).wait_send()
            row_recv(e, g, 1).wait_recv()

    def col_copy(e, g, side):
        return pltpu.make_async_remote_copy(
            src_ref=csend.at[e, g, side], dst_ref=crecv.at[e, g, 1 - side],
            send_sem=cs.at[e, g, side], recv_sem=cr.at[e, g, 1 - side],
            device_id={"lon": west if side == 0 else east}, device_id_type=MESH)

    def send_cols(e, g, ref):
        for r in range(rows):
            csend[e, g, 0, r:r + 1, :] = ref[r, PAD:PAD + 1, lanes(g)]
            csend[e, g, 1, r:r + 1, :] = ref[r, PAD + cols - 1:PAD + cols, lanes(g)]
        col_copy(e, g, 0).start()
        col_copy(e, g, 1).start()

    def wait_cols(e, g, ref):
        for side in (0, 1):
            col_copy(e, g, side).wait()
        for r in range(rows):
            ref[r, PAD - 1:PAD, lanes(g)] = crecv[e, g, 0, r:r + 1, :]
            ref[r, PAD + cols:PAD + cols + 1, lanes(g)] = crecv[e, g, 1, r:r + 1, :]

    def slab(c, r, g):
        return jnp.concatenate(
            [raw[c, i, pl.ds(r + 128 * rows * g, 128, stride=rows), :].T for i in range(tiles)], axis=0)

    def dcol(ref, r, g):
        return ref[r, PAD + 1:PAD + cols + 1, lanes(g)] - ref[r, PAD - 1:PAD + cols - 1, lanes(g)]

    def hrow(r, g):
        return hp[r, PAD:PAD + cols, lanes(g)]

    def frow(r, g):
        return fy[r, :, lanes(g)]

    def load_v(r, g):
        v = slab(2, r, g)
        fv[r, :, lanes(g)] = v
        fy[r, :, lanes(g)] = v * brep[r]

    def height(r, g, up, down):
        div = dcol(fxp, r, g) + down - up
        hp[r, PAD:PAD + cols, lanes(g)] = hrow(r, g) - 0.25 * div

    def wind(r, g, up, down, flux):
        f = fc[pl.ds(r, 1), :]
        u, v = fu[r, :, lanes(g)], fv[r, :, lanes(g)]
        un = u + 0.5 * (f * v - 0.5 * dcol(hp, r, g))
        vn = v - 0.5 * (f * u + 0.5 * (down - up))
        fu[r, :, lanes(g)] = un
        fv[r, :, lanes(g)] = vn
        if flux:
            b = brep[r]
            fxp[r, PAD:PAD + cols, lanes(g)] = un * b
            fy[r, :, lanes(g)] = vn * b

    def edges_height(e, g):
        wait_rows(e, g)
        height(0, g, rbuf[e, 0, :, lanes(g)], frow(1, g))
        height(last, g, frow(last - 1, g), rbuf[e, 1, :, lanes(g)])
        send_rows(e + 1, g)

    def inner_height(g):
        @pl.loop(1, last)
        def _(r):
            height(r, g, frow(r - 1, g), frow(r + 1, g))

    def inner_wind(g, flux):
        @pl.loop(1, last)
        def _(r):
            wind(r, g, hrow(r - 1, g), hrow(r + 1, g), flux)

    def edges_wind(e, g, flux):
        wait_rows(e, g)
        wind(0, g, rbuf[e, 0, :, lanes(g)], hrow(1, g), flux)
        wind(last, g, hrow(last - 1, g), rbuf[e, 1, :, lanes(g)], flux)

    for load in loads[2]:
        load.wait()
    for g in range(groups):
        for r in (0, last):
            load_v(r, g)
        if g == 0:
            pl.semaphore_wait(barrier, peers + 1)
        send_rows(0, g)
    for load in loads[1]:
        load.wait()
    for g in range(groups):
        for r in range(rows):
            u = slab(1, r, g)
            fu[r, :, lanes(g)] = u
            fxp[r, PAD:PAD + cols, lanes(g)] = u * brep[r]
        send_cols(0, g, fxp)
        for r in range(1, last):
            load_v(r, g)
        if g == 0:
            for load in loads[0]:
                load.wait()
        for r in range(rows):
            hp[r, PAD:PAD + cols, lanes(g)] = slab(0, r, g)
        wait_cols(0, g, fxp)
        edges_height(0, g)
        inner_height(g)
        send_cols(1, g, hp)
    for g in range(groups):
        wait_cols(1, g, hp)
        inner_wind(g, True)
        edges_wind(1, g, True)
        send_rows(2, g)
        send_cols(2, g, fxp)
    for g in range(groups):
        wait_cols(2, g, fxp)
        inner_height(g)
        edges_height(2, g)
        send_cols(3, g, hp)

    for load in small[1:]:
        load.wait()
    slots = hx.shape[0]
    bits = cols.bit_length() - 1
    if cols == 1 << bits:
        cell_row, cell_col = (lambda c: lax.shift_right_logical(c, bits)), (lambda c: c & (cols - 1))
    else:
        cell_row, cell_col = (lambda c: lax.div(c, cols)), (lambda c: lax.rem(c, cols))

    @pl.loop(0, slots // 8)
    def _(t):
        got = []
        for k in range(8):
            cell = index[0, t * 8 + k]
            got.append(hp[cell_row(cell), pl.ds(PAD + cell_col(cell), 1), :])
        hx[pl.ds(t * 8, 8), :] = jnp.concatenate(got, axis=0)

    x = hx[...]
    info = jnp.concatenate([value[...], sd[...], jnp.zeros((6, slots), jnp.float32)], axis=0).T
    sigma = info[:, 1:2] * (math.sqrt(slots * nlon * nlat) / 16.0)
    valid = (lax.broadcasted_iota(jnp.int32, (slots, 1), 0) < count[0, 0]).astype(jnp.float32)
    mean = jnp.sum(x, axis=1, keepdims=True) * (1.0 / members)
    yp = (x - mean) * (valid / (math.sqrt(members - 1) * sigma))
    innov = (info[:, 0:1] - mean) * (valid / sigma)
    proj = jnp.sum(yp * innov, axis=0, keepdims=True)
    hx[...] = yp
    yt[...] = yp.T

    mine = pl.ds(pl.multiple_of(core * half, half), half)
    theirs = pl.ds(pl.multiple_of((1 - core) * half, half), half)

    def guard(cond, run):
        if owners == peers:
            run()
        else:
            pl.when(cond)(run)

    def gram_rows(where):
        part[where, :] = jnp.dot(yt[where, :], hx[...], precision=lax.Precision.HIGHEST,
                                 preferred_element_type=jnp.float32)

    def put_proj():
        part[members - 2:members - 1, 0:half] = proj[:, :half]
        part[members - 1:members, 0:half] = proj[:, half:]

    first = pltpu.make_async_remote_copy(
        src_ref=part.at[theirs], dst_ref=other, send_sem=ps, recv_sem=pr,
        device_id=partner, device_id_type=MESH)
    gram_rows(theirs)
    pl.when(core == 0)(put_proj)
    first.start()
    gram_rows(mine)
    pl.when(core == 1)(put_proj)
    first.wait()
    acc[...] = part[mine, :] + other[...]

    def scatter(p, frm):
        return pltpu.make_async_remote_copy(
            src_ref=acc.at[pl.ds(pl.multiple_of(p * chunk, chunk), chunk)], dst_ref=parts.at[frm],
            send_sem=ss.at[p], recv_sem=sr.at[frm], device_id=device(p), device_id_type=MESH)

    def arrive(frm):
        return pltpu.make_async_remote_copy(
            src_ref=parts.at[frm], dst_ref=parts.at[frm],
            send_sem=ss.at[0], recv_sem=sr.at[frm], device_id=device(frm), device_id_type=MESH)

    @pl.loop(1, peers)
    def _(d):
        p = lax.rem(me + d, peers)
        guard(p < owners, lambda: scatter(p, me).start())

    for g in range(groups):
        wait_cols(3, g, hp)
        inner_wind(g, False)

    def forward(p):
        return pltpu.make_async_remote_copy(
            src_ref=whole.at[p], dst_ref=back.at[p], send_sem=qs.at[p], recv_sem=qr.at[p],
            device_id=partner, device_id_type=MESH)

    def collect():
        total = acc[pl.ds(pl.multiple_of(me * chunk, chunk), chunk), :]

        def body(d, total):
            frm = lax.rem(me + d, peers)
            arrive(frm).wait_recv()
            return total + parts[frm]
        whole[me] = lax.fori_loop(1, peers, body, total)

    guard(me < owners, collect)

    def spread(p, frm):
        return pltpu.make_async_remote_copy(
            src_ref=whole.at[frm], dst_ref=whole.at[frm],
            send_sem=gs.at[p], recv_sem=gr.at[frm], device_id=device(p), device_id_type=MESH)

    def send_all():
        @pl.loop(1, peers)
        def _(d):
            p = lax.rem(me + d, peers)
            spread(p, me).start()
        forward(me).start()

    guard(me < owners, send_all)
    for g in range(groups):
        edges_wind(3, g, False)

    @pl.loop(1, peers)
    def _(d):
        p = lax.rem(me + d, peers)

        def relay():
            spread(p, p).wait_recv()
            forward(p).start()

        guard(p < owners, relay)

    @pl.loop(1, peers)
    def _(d):
        p = lax.rem(me + d, peers)
        guard(p < owners, lambda: scatter(p, me).wait_send())

    def sent_all():
        @pl.loop(1, peers)
        def _(d):
            p = lax.rem(me + d, peers)
            spread(p, me).wait_send()

    guard(me < owners, sent_all)
    out[mine, :] = whole[...].reshape(half, members)

    @pl.loop(0, owners)
    def _(p):
        forward(p).wait()

    out[theirs, :] = back[...].reshape(half, members)


def forecast(nlon, nlat, state, bathymetry, obs_index, obs_count, obs_value, obs_sd):
    _, members, rows, cols = state.shape
    slots = obs_index.shape[2]
    f32, dma = jnp.float32, pltpu.SemaphoreType.DMA
    field = jax.ShapeDtypeStruct((rows, cols, members), f32)
    vmem, hbm = pl.BlockSpec(memory_space=pltpu.VMEM), pl.BlockSpec(memory_space=pltpu.HBM)
    half, peers, groups = members // 2, nlon // 2 * nlat, members // 128
    owners = min(peers, half // 8)
    chunk = half // owners
    return pl.pallas_call(
        functools.partial(forecast_kernel, nlon, nlat, members, rows, cols),
        out_shape=[jax.ShapeDtypeStruct((rows, cols + 2 * PAD, members), f32), field, field, jax.ShapeDtypeStruct((members, members), f32)],
        in_specs=[hbm] * 6,
        out_specs=[vmem] * 4,
        scratch_shapes=[
            pltpu.VMEM((3, cols // 128, members * rows, 128), f32),
            pltpu.VMEM((rows, cols + 2 * PAD, members), f32),
            pltpu.VMEM((rows, cols, members), f32),
            pltpu.VMEM((rows, cols, 128), f32),
            pltpu.VMEM((4, 2, cols, members), f32),
            pltpu.VMEM((4, groups, 2, rows, 128), f32),
            pltpu.VMEM((4, groups, 2, rows, 128), f32),
            pltpu.VMEM((slots, members), f32),
            pltpu.VMEM((rows, cols), f32),
            pltpu.SMEM((1, slots), jnp.int32),
            pltpu.SMEM((1, 1), jnp.int32),
            pltpu.VMEM((1, slots), f32),
            pltpu.VMEM((1, slots), f32),
            pltpu.VMEM((rows, 128), f32),
            pltpu.VMEM((members, slots), f32),
            pltpu.VMEM((members, members), f32),
            pltpu.VMEM((half, members), f32), pltpu.VMEM((half, members), f32),
            pltpu.VMEM((peers, chunk, members), f32), pltpu.VMEM((owners, chunk, members), f32),
            pltpu.VMEM((owners, chunk, members), f32),
            dma((3, cols // 128)), dma((5,)),
            dma((4, groups, 2)), dma((4, groups, 2)), dma((4, groups, 2)), dma((4, groups, 2)),
            dma, dma, dma((peers,)), dma((peers,)), dma((peers,)), dma((peers,)), dma((owners,)), dma((owners,)),
        ],
        compiler_params=pltpu.CompilerParams(
            collective_id=0, has_side_effects=True, vmem_limit_bytes=30 * 2**20),
    )(*(x if x.size == 1 else pltpu.with_memory_space_constraint(x, pltpu.HBM) for x in (
        state.reshape(3, members * rows, cols), bathymetry, obs_index.reshape(1, slots), obs_count,
        obs_value.reshape(1, slots), obs_sd.reshape(1, slots))))


def split(x):
    hi = x.astype(jnp.bfloat16)
    return hi, (x - hi.astype(jnp.float32)).astype(jnp.bfloat16)


def recip(x):
    r = pl.reciprocal(x, approx=True)
    return r * (2.0 - x * r)


def tree_sum(terms):
    while len(terms) > 1:
        terms = [sum(terms[i:i + 2][1:], terms[i]) for i in range(0, len(terms), 2)]
    return terms[0]


def invert_block(x):
    size, step = x.shape[0], 16
    lane = lax.broadcasted_iota(jnp.int32, (step, size), 1)
    sub = lax.broadcasted_iota(jnp.int32, (step, size), 0)
    blocks = [x[i:i + step, :] for i in range(0, size, step)]
    done = []
    for t in range(size // step):
        base = step * t
        row = blocks[t]
        inpanel = (lane >= base) & (lane < base + step)
        diag = [jnp.broadcast_to(row[:, base + q:base + q + 1], (step, size)) for q in range(step)]
        aug = jnp.where(inpanel, jnp.where(lane == base + sub, 1.0, 0.0), row)
        inv = jnp.zeros((step, size), jnp.float32)
        piv = jnp.ones((step, size), jnp.float32)
        for k in range(0, step, 2):
            d0, d1 = diag[k], diag[k + 1]
            a, b, c = d0[k:k + 1, :], d1[k:k + 1, :], d1[k + 1:k + 2, :]
            det = a * c - b * b
            ra, rdet = recip(a), recip(det)
            ratio, rp = b * ra, a * rdet
            inv = jnp.where(sub == k, ra, jnp.where(sub == k + 1, rp, inv))
            piv = jnp.where(sub == k, a, jnp.where(sub == k + 1, det * ra, piv))
            l0 = jnp.where(sub > k, d0 * ra, 0.0)
            l1 = jnp.where(sub > k + 1, (d1 - l0 * b) * rp, 0.0)

            def eliminate(z):
                first = z[k:k + 1, :]
                second = z[k + 1:k + 2, :] - ratio * first
                return z - (l0 * first + l1 * second)

            for q in range(k + 2, step):
                diag[q] = eliminate(diag[q])
            aug = eliminate(aug)
        done.append(jnp.where(lane < base + step, aug, 0.0) * lax.rsqrt(piv))
        if base + step < size:
            factor = (aug * inv).T
            for s in range(t + 1, size // step):
                fac = factor[step * s:step * (s + 1), :]
                terms = [fac[:, k:k + 1] * aug[k:k + 1, :] for k in range(step)]
                blocks[s] = jnp.where(inpanel, 0.0, blocks[s]) - tree_sum(terms)
    return jnp.concatenate(done, axis=0)


def dot_at(x, y, dims):
    return lax.dot_general(x, y, (dims, ((), ())), precision=lax.Precision.HIGHEST,
                           preferred_element_type=jnp.float32)


def invert(gram):
    size = gram.shape[0]
    half = size // 2
    i = lax.broadcasted_iota(jnp.int32, (half, half), 0)
    j = lax.broadcasted_iota(jnp.int32, (half, half), 1)
    eye = (i == j).astype(jnp.float32)
    m1 = invert_block(gram[:half, :half] + eye)
    side = dot_at(m1, gram[:half, half:], ((1,), (0,)))
    st = side.T
    m2 = invert_block(gram[half:, half:] + eye - dot_at(st, side, ((1,), (0,))))
    low = -dot_at(m2, dot_at(st, m1, ((1,), (0,))), ((1,), (0,)))
    top = jnp.concatenate([m1, jnp.zeros((half, half), jnp.float32)], axis=1)
    return jnp.concatenate([top, jnp.concatenate([low, m2], axis=1)], axis=0)


def analysis_kernel(members, gram, hp, fu, fv, out, hi, lo, buf, sem):
    g = gram[...]
    half = members // 2
    proj = jnp.concatenate([g[members - 2:members - 1, :half], g[members - 1:members, :half]], axis=1)
    inv = invert(g)
    part = jnp.sum(inv * proj, axis=1, keepdims=True)
    weights = jnp.sum(inv * part, axis=0, keepdims=True)
    t = inv + weights * (1.0 / math.sqrt(members - 1))
    t = t + (1.0 - jnp.sum(t, axis=1, keepdims=True)) * (1.0 / members)
    a, b = split(t)
    hi[...] = a
    lo[...] = b
    dims = (((1,), (1,)), ((), ()))
    dot = functools.partial(lax.dot_general, dimension_numbers=dims, preferred_element_type=jnp.float32)
    rows, cols, _ = fu.shape
    copies = []
    for c, ref in enumerate((hp, fu, fv)):
        skip = PAD if c == 0 else 0
        for i in range(cols // 128):
            for r in range(0, rows, 2):
                x = jnp.concatenate(
                    [ref[r + k, skip + 128 * i:skip + 128 * (i + 1), :] for k in range(2)], axis=0)
                a, b = split(x)
                mixed = dot(hi[...], a) + dot(hi[...], b) + dot(lo[...], a)
                for k in range(2):
                    buf[c, i, pl.ds(r + k, members, stride=rows), :] = mixed[:, 128 * k:128 * (k + 1)]
            copy = pltpu.make_async_copy(buf.at[c, i], out.at[c, :, pl.ds(128 * i, 128)], sem.at[c, i])
            copy.start()
            copies.append(copy)
    for copy in copies:
        copy.wait()


def analyse(gram, fields):
    rows, cols, members = fields[1].shape
    tiles = cols // 128
    vmem = pl.BlockSpec(memory_space=pltpu.VMEM)
    out = pl.pallas_call(
        functools.partial(analysis_kernel, members),
        out_shape=jax.ShapeDtypeStruct((3, members * rows, cols), jnp.float32),
        in_specs=[vmem] * 4,
        out_specs=pl.BlockSpec(memory_space=pltpu.HBM),
        scratch_shapes=[pltpu.VMEM((members, members), jnp.bfloat16)] * 2 + [
            pltpu.VMEM((3, tiles, members * rows, 128), jnp.float32),
            pltpu.SemaphoreType.DMA((3, tiles))],
        compiler_params=pltpu.CompilerParams(vmem_limit_bytes=20 * 2**20),
    )(gram, *fields)
    return out.reshape(3, members, rows, cols)


def shards(nlon, nlat, state, bathymetry, obs_index, obs_count, obs_value, obs_sd):
    h, u, v, gram = forecast(nlon, nlat, state, bathymetry, obs_index, obs_count, obs_value, obs_sd)
    return analyse(gram, (h, u, v))


def solution(mesh):
    return jax.shard_map(
        functools.partial(shards, mesh.shape["lon"], mesh.shape["lat"]),
        mesh=mesh,
        in_specs=(
            P(None, None, "lat", "lon"),
            P("lat", "lon"),
            P("lat", "lon", None),
            P("lat", "lon"),
            P("lat", "lon", None),
            P("lat", "lon", None),
        ),
        out_specs=P(None, None, "lat", "lon"),
        check_vma=False,
    )
```
